32 devices in a mesh: row: 8 (over z, x), col: 4 (over y, core).
Axes of the slice: x: 2, y: 2, z: 4, core: 2. Of those that a mesh axis runs over, the one named last changes fastest.
Arguments:
- potential: float32 [16, 16, 512], P('row', 'col'), may hold values from -6 to 6
- basis: bfloat16 [16, 16, 384, 512], P('row', 'col'), may hold values from -6 to 6
- hamiltonian: bfloat16 [3072, 3072], P('row', 'col'), may hold values from -0.109375 to 0.109375
- density: bfloat16 [2, 3072, 3072], P(None, 'row', 'col'), may hold values from -6 to 6
- hmask: int32 [24, 24], replicated, may hold values from 0 to 1, as said below
- pmask: int32 [24, 24], replicated, may hold values from 0 to 1, as said below
Outputs:
- propagated: bfloat16 [2, 3072, 3072], P(None, 'row', 'col')
The draws below stay inside these ranges and needn't reach their ends.
Inputs may be any that keep to these rules, and one draw needn't show every extreme that they name: hmask[I, I] is always 1; every other block is 1 with probability 1/2, independently. pmask follows the same law as hmask, drawn independently.
All inputs are finite; a program needn't handle non-finite values.
Results may differ from the reference program's by a relative error of at most 0.0062.
Values may be sent and summed in bfloat16 or wider, within the bound.
No kernel may reach another device: no remote copies, remote signals or barrier semaphores. Data moves between devices by JAX's collectives and lax.ppermute only.
A program may use at most 64 MiB of HBM per device.

```python
import jax
import jax.numpy as jnp
from jax import lax

BLK = 128
KB = 3
CX = 2
GZ = 512
NBLK = 24
ORDER = 3072
GX = 16
GY = 16
N_ROW = 8


def random_pattern(key):
    index = jnp.arange(NBLK, dtype=jnp.int32)
    same = index[:, None] == index[None, :]
    coins = jax.random.randint(key, (NBLK, NBLK), 0, 2)
    keep = (coins > 0) | same
    return keep.astype(jnp.int32)


def draw_hmask(key, part):
    return random_pattern(jax.random.fold_in(key, 11))


def draw_pmask(key, part):
    return random_pattern(jax.random.fold_in(key, 23))


def levels(rng, dims, split, least, top_value):
    def one(position, shards_of):
        draws = jax.random.uniform(jax.random.fold_in(jax.random.fold_in(rng, 6), position), (shards_of,), jnp.float32, least / len(split), top_value / len(split))
        return jnp.repeat(jnp.exp(draws), dims[position] // shards_of).reshape((-1,) + (1,) * (len(dims) - position - 1))

    loudness = one(*split[0])
    for cut in split[1:]:
        loudness = loudness * one(*cut)
    return loudness


def gaussian(stream_key, extent, deviation, bound, pieces=(), held_as=jnp.bfloat16):
    result = deviation * jax.random.normal(stream_key, extent, jnp.float32)
    if pieces:
        result = result * levels(stream_key, extent, pieces, -0.22, 0.18)
    return jnp.clip(result, -bound, bound).astype(held_as)


def setup_inputs(seed: int = 0) -> dict:
    key_of = jax.random.split(jax.random.key(seed), 7)
    return {
        "potential": gaussian(key_of[0], (GX, GY, GZ), 1.0, 6.0, ((0, 8), (1, 4)), jnp.float32),
        "basis": gaussian(key_of[1], (GX, GY, KB * BLK, GZ), 1.0, 6.0, ((0, 8), (1, 4))),
        "hamiltonian": gaussian(key_of[2], (ORDER, ORDER), ORDER ** -0.5, 0.109375, ((0, 8), (1, 4))),
        "density": gaussian(key_of[3], (2, ORDER, ORDER), 1.0, 6.0, ((1, 8), (2, 4))),
        "hmask": draw_hmask(jax.random.fold_in(key_of[6], 71), 0),
        "pmask": draw_pmask(jax.random.fold_in(key_of[6], 71), 0),
    }


KAPPA = 0.4
TIME_STEP = 0.5


def screened(potential):
    padded = jnp.pad(potential, 1)
    beside = padded[2:, 1:-1, 1:-1] + padded[:-2, 1:-1, 1:-1]
    beside = beside + padded[1:-1, 2:, 1:-1] + padded[1:-1, :-2, 1:-1]
    beside = beside + padded[1:-1, 1:-1, 2:] + padded[1:-1, 1:-1, :-2]
    return potential + KAPPA * (beside - 6.0 * potential)


def integrate(packed):
    slab_values, table = packed
    weighted = (table.astype(jnp.float32) * slab_values[:, :, None, None, :]).astype(jnp.bfloat16)
    weighted = lax.optimization_barrier(weighted)
    return jnp.einsum("xykaz,xykbz->kab", weighted.astype(jnp.float32), table.astype(jnp.float32))


def reference(potential, basis, hamiltonian, density, hmask, pmask):
    effective = screened(potential)
    slab_v = effective.reshape(N_ROW, CX, GY, GZ)
    slab_b = basis.reshape(N_ROW, CX, GY, KB, BLK, GZ)
    blocks = lax.map(integrate, (slab_v, slab_b))
    factor = float(BLK * CX * GY * GZ) ** -0.5
    potential_blocks = (blocks * factor).reshape(NBLK, BLK, BLK).astype(jnp.bfloat16)
    masked_h = (hamiltonian.reshape(NBLK, BLK, NBLK, BLK) * hmask[:, None, :, None].astype(jnp.bfloat16)).reshape(ORDER, ORDER)
    pattern = pmask[None, :, None, :, None]
    masked_p = (density.reshape(2, NBLK, BLK, NBLK, BLK) * pattern.astype(jnp.bfloat16)).reshape(2, ORDER, ORDER)

    def apply(operand):
        remote = jnp.stack([jnp.dot(masked_h, operand[0], preferred_element_type=jnp.float32),
                            jnp.dot(masked_h, operand[1], preferred_element_type=jnp.float32)])
        diagonal_term = jnp.einsum("kab,skbc->skac", potential_blocks.astype(jnp.float32),
                                   operand.reshape(2, NBLK, BLK, ORDER).astype(jnp.float32))
        return remote + diagonal_term.reshape(2, ORDER, ORDER)

    first = apply(masked_p)
    first_rounded = first.astype(jnp.bfloat16)
    second = apply(first_rounded)
    base = masked_p.astype(jnp.float32)
    half_square = 0.5 * TIME_STEP * TIME_STEP
    real_part = base[0] + TIME_STEP * first[1] - half_square * second[0]
    imag_part = base[1] - TIME_STEP * first[0] - half_square * second[1]
    stacked = jnp.stack([real_part, imag_part]).reshape(2, NBLK, BLK, NBLK, BLK) * pattern.astype(jnp.float32)
    return stacked.reshape(2, ORDER, ORDER).astype(jnp.bfloat16)
```

```python
import functools

import jax
import jax.numpy as jnp
from jax import lax
from jax.experimental import pallas as pl
from jax.experimental.pallas import tpu as pltpu
from jax.sharding import PartitionSpec as P

BLK = 128
KAPPA = 0.4
TIME_STEP = 0.5
BF16 = jnp.bfloat16
F32 = jnp.float32
VMEM_BYTES = 48 * 1024 * 1024

SMEM_SPEC = pl.BlockSpec(memory_space=pltpu.SMEM)
VMEM_SPEC = pl.BlockSpec(memory_space=pltpu.VMEM)


def call(body, scalars, arrays, outs, scratch=(), flops=0):
    moved = sum(a.size * a.dtype.itemsize for a in arrays)
    moved += sum(o.size * o.dtype.itemsize for o in outs)
    return pl.pallas_call(
        body,
        out_shape=tuple(outs),
        in_specs=[SMEM_SPEC] * len(scalars) + [VMEM_SPEC] * len(arrays),
        out_specs=tuple(VMEM_SPEC for _ in outs),
        scratch_shapes=list(scratch),
        compiler_params=pltpu.CompilerParams(vmem_limit_bytes=VMEM_BYTES),
        cost_estimate=pl.CostEstimate(flops=flops, bytes_accessed=moved, transcendentals=0),
    )(*scalars, *arrays)


def shape(*dims, dtype=BF16):
    return jax.ShapeDtypeStruct(dims, dtype)


def pack_kernel(cap, kb, jb, info, hmask, h, packed):
    row, col = info[0], info[1]
    place = jnp.int32(0)
    for k in range(kb):
        for j in range(jb):
            keep = (hmask[row * kb + k, col * jb + j] != 0) & (place < cap)

            @pl.when(keep)
            def _(k=k, j=j, place=place):
                packed[place] = h[k * BLK : (k + 1) * BLK, j * BLK : (j + 1) * BLK]

            place = place + keep.astype(jnp.int32)


def turn_kernel(zs, kb, jb, info, pmask, p, *rest):
    pieces, turned = rest[:-1], rest[-1]
    row, col = info[0], info[1]
    z = row // 2
    wide = BLK // zs
    for k in range(kb):
        for j in range(jb):
            keep = pmask[row * kb + k, col * jb + j] != 0
            for part in range(2):
                here = p[part, k * BLK : (k + 1) * BLK, j * BLK : (j + 1) * BLK]
                here = jnp.where(keep, here, jnp.zeros_like(here)).T
                top = (part * jb + j) * BLK
                turned[top : top + BLK, k * BLK : (k + 1) * BLK] = here
    for s in range(zs):
        start = pl.multiple_of((z ^ s) * wide, wide)
        for i in range(2 * jb):
            pieces[s][i * wide : (i + 1) * wide, :] = turned[pl.ds(i * BLK + start, wide), :]


def return_kernel(zs, kb, jb, info, pmask, *rest):
    pieces, out, turned = rest[:zs], rest[zs], rest[zs + 1]
    row, col = info[0], info[1]
    z = row // 2
    wide = BLK // zs
    for s in range(zs):
        start = pl.multiple_of((z ^ s) * wide, wide)
        for i in range(2 * jb):
            turned[pl.ds(i * BLK + start, wide), :] = pieces[s][i * wide : (i + 1) * wide, :]
    for k in range(kb):
        for j in range(jb):
            keep = pmask[row * kb + k, col * jb + j] != 0
            for part in range(2):
                top = (part * jb + j) * BLK
                here = turned[top : top + BLK, k * BLK : (k + 1) * BLK]
                here = jnp.where(keep, here, jnp.zeros_like(here)).T
                out[part, k * BLK : (k + 1) * BLK, j * BLK : (j + 1) * BLK] = here


def join_kernel(zs, side, info, *rest):
    out = rest[-1]
    z, x = info[0] // 2, info[0] % 2
    for s in range(zs):
        for other in range(2):
            start = pl.multiple_of((2 * (z ^ s) + (x ^ other)) * side, side)
            out[:, pl.ds(start, side)] = rest[2 * s + other][...]


def first_kernel(s, kb, jb, info, hmask, joined, diagonal, *rest):
    packed, (dense, first) = rest[:-2], rest[-2:]
    row = info[0] ^ (2 * s)
    for m in range(len(packed)):
        col = info[1] ^ m
        place = jnp.int32(0)
        for k in range(kb):
            for j in range(jb):
                block_col = col * jb + j
                keep = hmask[row * kb + k, block_col] != 0
                start = pl.multiple_of(block_col * BLK, BLK)

                @pl.when(keep)
                def _(k=k, m=m, place=place, start=start):
                    dense[k * BLK : (k + 1) * BLK, pl.ds(start, BLK)] = packed[m][place]

                @pl.when(jnp.logical_not(keep))
                def _(k=k, start=start):
                    dense[k * BLK : (k + 1) * BLK, pl.ds(start, BLK)] = jnp.zeros((BLK, BLK), BF16)

                place = place + keep.astype(jnp.int32)
    for k in range(kb):
        rows = pl.ds(k * BLK, BLK)
        columns = pl.ds(pl.multiple_of((row * kb + k) * BLK, BLK), BLK)
        both = dense[rows, columns].astype(F32) + diagonal[k * BLK : (k + 1) * BLK, :].astype(F32)
        dense[rows, columns] = both.astype(BF16)
    first[...] = lax.dot_general(
        joined[...], dense[...], (((1,), (1,)), ((), ())), preferred_element_type=F32
    ).astype(BF16)


def second_kernel(count, joined, *rest):
    half_square = 0.5 * TIME_STEP * TIME_STEP
    dense, density, first, outs = (rest[i * count : (i + 1) * count] for i in range(4))
    for i in range(count):
        second = lax.dot_general(
            joined[...], dense[i][...], (((1,), (1,)), ((), ())), preferred_element_type=F32
        )
        half = second.shape[0] // 2
        real, imag = slice(0, half), slice(half, 2 * half)
        outs[i][real, :] = (
            density[i][real, :].astype(F32)
            + TIME_STEP * first[i][imag, :].astype(F32)
            - half_square * second[real, :]
        ).astype(BF16)
        outs[i][imag, :] = (
            density[i][imag, :].astype(F32)
            - TIME_STEP * first[i][real, :].astype(F32)
            - half_square * second[imag, :]
        ).astype(BF16)


def swap_row(value, bits):
    count = lax.axis_size("row")
    return lax.ppermute(value, "row", [(i, i ^ bits) for i in range(count)])


def swap_col(value, bits):
    count = lax.axis_size("col")
    return lax.ppermute(value, "col", [(i, i ^ bits) for i in range(count)])


def from_line(own, z):
    zs = lax.axis_size("row") // 2
    if zs != 4:
        return [own] + [swap_row(own, 2 * s) for s in range(1, zs)]

    def along(value, pairs):
        return lax.ppermute(value, "row", [(2 * a + x, 2 * b + x) for a, b in pairs for x in range(2)])

    middle, outward = [(1, 2), (2, 1)], [(1, 0), (2, 3)]
    beside = swap_row(own, 2)
    across = along(own, middle)
    across_beside = along(beside, middle)
    out_near = along(across, outward)
    out_far = along(across_beside, outward)
    inner = (z == 1) | (z == 2)
    return [
        own,
        beside,
        jnp.where(inner, across_beside, out_near),
        jnp.where(inner, across, out_far),
    ]


def effective_potential(potential):
    def beyond(axis, dim):
        count = lax.axis_size(axis)
        forward = [(i, i + 1) for i in range(count - 1)]
        backward = [(target, source) for source, target in forward]
        last = potential.shape[dim] - 1
        low = lax.ppermute(lax.slice_in_dim(potential, last, None, axis=dim), axis, forward)
        high = lax.ppermute(lax.slice_in_dim(potential, 0, 1, axis=dim), axis, backward)
        return jnp.concatenate([low, potential, high], axis=dim)

    in_x, in_y = beyond("row", 0), beyond("col", 1)
    in_z = jnp.pad(potential, ((0, 0), (0, 0), (1, 1)))
    beside = in_x[2:] + in_x[:-2]
    beside = beside + in_y[:, 2:] + in_y[:, :-2]
    beside = beside + in_z[:, :, 2:] + in_z[:, :, :-2]
    return potential + KAPPA * (beside - 6.0 * potential)


def potential_blocks(potential, basis):
    width_x, width_y, depth_z = potential.shape
    kb = basis.shape[2] // BLK
    effective = effective_potential(potential)
    weighted = (basis * effective[:, :, None, :]).astype(BF16)
    partial = jnp.einsum(
        "xykaz,xykbz->kab",
        weighted.reshape(width_x, width_y, kb, BLK, depth_z),
        basis.reshape(width_x, width_y, kb, BLK, depth_z),
        preferred_element_type=F32,
    ).reshape(kb * BLK, BLK)
    half = kb * BLK // 2
    low, high = partial[:half], partial[half:]
    even = lax.axis_index("col") % 2 == 0
    mine = jnp.where(even, low, high) + swap_col(jnp.where(even, high, low), 1)
    total = mine
    for t in range(1, lax.axis_size("col") // 2):
        total = total + swap_col(mine, 2 * t)
    factor = float(BLK * width_x * width_y * depth_z * lax.axis_size("col")) ** (-0.5)
    return (total * factor).astype(BF16)


def shards(potential, basis, hamiltonian, density, hmask, pmask):
    row, col = lax.axis_index("row"), lax.axis_index("col")
    info = jnp.stack([row, col]).astype(jnp.int32)
    z, core = row // 2, col % 2
    zs = lax.axis_size("row") // 2
    cols = lax.axis_size("col")
    side, across = hamiltonian.shape
    order = side * lax.axis_size("row")
    kb, jb = side // BLK, across // BLK
    cap = kb * jb
    wide = 2 * across // zs

    (packed,) = call(
        functools.partial(pack_kernel, cap, kb, jb), [info, hmask], [hamiltonian], [shape(cap, BLK, BLK)]
    )
    lines = from_line(packed, z)

    pieces = call(
        functools.partial(turn_kernel, zs, kb, jb),
        [info, pmask],
        [density],
        [shape(wide, side)] * zs,
        scratch=[pltpu.VMEM((2 * across, side), BF16)],
    )

    def join(same, other):
        both = [piece for pair in zip(same, other) for piece in pair]
        return call(functools.partial(join_kernel, zs, side), [info], both, [shape(wide, order)])[0]

    mine = [pieces[s] if s == 0 else swap_row(pieces[s], 2 * s) for s in range(zs)]
    theirs = [swap_row(piece, 1) for piece in mine]
    joined = join(mine, theirs)

    own_half = potential_blocks(potential, basis)
    halves = [own_half] + [swap_row(own_half, 2 * s) for s in range(1, zs)]
    stacked = jnp.stack(halves)
    beside = swap_col(stacked, 1)
    diagonal = jnp.concatenate(
        [jnp.where(core == 0, stacked, beside), jnp.where(core == 0, beside, stacked)], axis=1
    )

    dense, first = [], []
    for s in range(zs):
        blocks = []
        for t in range(cols // 2):
            here = lines[s] if t == 0 else swap_col(lines[s], 2 * t)
            blocks += [here, swap_col(here, 1)]
        d, f = call(
            functools.partial(first_kernel, s, kb, jb),
            [info, hmask],
            [joined, diagonal[s], *blocks],
            [shape(side, order), shape(wide, side)],
            flops=2 * side * order * wide,
        )
        dense.append(d)
        first.append(f)
    first_joined = join(first, [swap_row(f, 1) for f in first])

    result = [None] * zs
    for slots in [[s] for s in range(zs - 1, -1, -1)]:
        outs = call(
            functools.partial(second_kernel, len(slots)),
            [],
            [first_joined]
            + [dense[s] for s in slots]
            + [mine[s] for s in slots]
            + [first[s] for s in slots],
            [shape(wide, side)] * len(slots),
            flops=2 * side * order * wide * len(slots),
        )
        for s, out in zip(slots, outs):
            result[s] = out if s == 0 else swap_row(out, 2 * s)

    return call(
        functools.partial(return_kernel, zs, kb, jb),
        [info, pmask],
        result,
        [shape(2, side, across)],
        scratch=[pltpu.VMEM((2 * across, side), BF16)],
    )[0]


def extended_2(block, sides, width):
    for axis, dim in sides:
        count = lax.axis_size(axis)
        forward = [(i, i + 1) for i in range(count - 1)]
        backward = [(target, source) for source, target in forward]
        low = lax.ppermute(
            lax.slice_in_dim(block, block.shape[dim] - width, None, axis=dim), axis, forward
        )
        high = lax.ppermute(lax.slice_in_dim(block, 0, width, axis=dim), axis, backward)
        block = jnp.concatenate([low, block, high], axis=dim)
    return block


def gathered(potential, basis, hamiltonian, density, hmask, pmask):
    width_x, width_y, depth_z = potential.shape
    extended = extended_2(potential, (("row", 0), ("col", 1)), 1)
    padded = jnp.pad(extended, ((0, 0), (0, 0), (1, 1)))
    beside = padded[2:, 1:-1, 1:-1] + padded[:-2, 1:-1, 1:-1]
    beside = beside + padded[1:-1, 2:, 1:-1] + padded[1:-1, :-2, 1:-1]
    beside = beside + padded[1:-1, 1:-1, 2:] + padded[1:-1, 1:-1, :-2]
    effective = potential + KAPPA * (beside - 6.0 * potential)
    blocks_here = basis.shape[2] // BLK
    weighted = (basis * effective[:, :, None, :]).astype(BF16)
    partial_blocks = jnp.einsum(
        "xykaz,xykbz->kab",
        weighted.reshape(width_x, width_y, blocks_here, BLK, depth_z),
        basis.reshape(width_x, width_y, blocks_here, BLK, depth_z),
        preferred_element_type=F32,
    )
    summed = lax.psum(partial_blocks, "col")
    factor = float(BLK * width_x * width_y * depth_z * lax.axis_size("col")) ** (-0.5)
    potential_blocks = (summed * factor).astype(BF16)
    block_total = hmask.shape[0]
    blocks_wide = block_total // lax.axis_size("col")
    row_start = lax.axis_index("row") * blocks_here
    col_start = lax.axis_index("col") * blocks_wide
    hpattern = lax.dynamic_slice(hmask, (row_start, col_start), (blocks_here, blocks_wide))
    ppattern = lax.dynamic_slice(pmask, (row_start, col_start), (blocks_here, blocks_wide))
    masked_h = (
        hamiltonian.reshape(blocks_here, BLK, blocks_wide, BLK)
        * hpattern[:, None, :, None].astype(BF16)
    ).reshape(blocks_here * BLK, blocks_wide * BLK)
    masked_p = (
        density.reshape(2, blocks_here, BLK, blocks_wide, BLK)
        * ppattern[None, :, None, :, None].astype(BF16)
    ).reshape(2, blocks_here * BLK, blocks_wide * BLK)

    def diagonal_term(operand):
        local = jnp.einsum(
            "kab,skbc->skac",
            potential_blocks,
            operand.reshape(2, blocks_here, BLK, operand.shape[2]),
            preferred_element_type=F32,
        )
        return local.reshape(2, blocks_here * BLK, operand.shape[2])

    def apply(operand):
        column_whole = lax.all_gather(operand, "row", axis=1, tiled=True)
        remote = jnp.einsum(
            "rk,skc->src",
            lax.all_gather(masked_h, "col", axis=1, tiled=True),
            column_whole,
            preferred_element_type=F32,
        )
        return remote + diagonal_term(operand)

    first = apply(masked_p)
    first_rounded = first.astype(BF16)
    second = apply(first_rounded)
    base = masked_p.astype(F32)
    half_square = 0.5 * TIME_STEP * TIME_STEP
    real_part = base[0] + TIME_STEP * first[1] - half_square * second[0]
    imag_part = base[1] - TIME_STEP * first[0] - half_square * second[1]
    stacked = jnp.stack([real_part, imag_part]).reshape(2, blocks_here, BLK, blocks_wide, BLK)
    stacked = stacked * ppattern[None, :, None, :, None].astype(F32)
    return stacked.reshape(2, blocks_here * BLK, blocks_wide * BLK).astype(BF16)


def solution(mesh):
    in_specs = (
        P("row", "col", None),
        P("row", "col", None, None),
        P("row", "col"),
        P(None, "row", "col"),
        P(),
        P(),
    )
    out_specs = P(None, "row", "col")
    body = shards if (mesh.shape["row"], mesh.shape["col"]) == (8, 4) else gathered
    return jax.shard_map(body, mesh=mesh, in_specs=in_specs, out_specs=out_specs, check_vma=False)
```

```python
import functools

import jax
import jax.numpy as jnp
from jax import lax
from jax.experimental import pallas as pl
from jax.experimental.pallas import tpu as pltpu
from jax.sharding import PartitionSpec as P

BLK = 128
KAPPA = 0.4
TIME_STEP = 0.5
BF16 = jnp.bfloat16
F32 = jnp.float32
VMEM_BYTES = 48 * 1024 * 1024

SMEM_SPEC = pl.BlockSpec(memory_space=pltpu.SMEM)
VMEM_SPEC = pl.BlockSpec(memory_space=pltpu.VMEM)


def call(body, scalars, arrays, outs, scratch=(), flops=0, weight=1):
    moved = sum(a.size * a.dtype.itemsize for a in arrays)
    moved += sum(o.size * o.dtype.itemsize for o in outs)
    return pl.pallas_call(
        body,
        out_shape=tuple(outs),
        in_specs=[SMEM_SPEC] * len(scalars) + [VMEM_SPEC] * len(arrays),
        out_specs=tuple(VMEM_SPEC for _ in outs),
        scratch_shapes=list(scratch),
        compiler_params=pltpu.CompilerParams(vmem_limit_bytes=VMEM_BYTES),
        cost_estimate=pl.CostEstimate(flops=flops, bytes_accessed=weight * moved, transcendentals=0),
    )(*scalars, *arrays)


def shape(*dims, dtype=BF16):
    return jax.ShapeDtypeStruct(dims, dtype)


def kept(mask, row, start, kb, width):
    place = jnp.int32(0)
    for k in range(kb):
        for j in range(width):
            keep = mask[row * kb + k, start + j] != 0
            yield k, j, keep, place
            place = place + keep.astype(jnp.int32)


def pack_kernel(cap, kb, jb, info, hmask, h, h_core, quarter, packed, slots):
    core = info[1] % 2
    for k, j, _, place in kept(hmask, info[0], (info[1] - core) * jb, kb, 2 * jb):
        columns = slice(j % jb * BLK, (j % jb + 1) * BLK)
        block = jnp.where(core == j // jb, h[k * BLK : (k + 1) * BLK, columns], h_core[k * BLK : (k + 1) * BLK, columns])
        here = jnp.clip(place - core * cap, -1, cap) + 1
        slots[pl.ds(pl.multiple_of(here * BLK, BLK), BLK), :] = block
    packed[: cap * BLK, :] = slots[BLK : (cap + 1) * BLK, :]
    packed[cap * BLK :, :] = quarter[...]


def turn_kernel(cap, zs, kb, jb, info, pmask, p, *rest):
    pieces, turned = rest[:-1], rest[-1]
    wide = BLK // zs
    for k, j, _, place in kept(pmask, info[0], info[1] * jb, kb, jb):
        for part in range(2):
            here = p[part, k * BLK : (k + 1) * BLK, j * BLK : (j + 1) * BLK]
            top = pl.multiple_of((2 * place + part) * BLK, BLK)
            turned[pl.ds(top, BLK), :] = here.T
    for s in range(zs):
        start = pl.multiple_of(((info[0] // 2) ^ s) * wide, wide)
        for i in range(2 * cap):
            pieces[s][i * wide : (i + 1) * wide, :] = turned[pl.ds(i * BLK + start, wide), :]


def return_kernel(cap, zs, kb, jb, info, pmask, p, *rest):
    pieces, out, turned = rest[:zs], rest[zs], rest[zs + 1]
    wide = BLK // zs
    for s in range(zs):
        start = pl.multiple_of(((info[0] // 2) ^ s) * wide, wide)
        for i in range(2 * cap):
            turned[pl.ds(i * BLK + start, wide), :] = pieces[s][i * wide : (i + 1) * wide, :]
    for k, j, keep, place in kept(pmask, info[0], info[1] * jb, kb, jb):
        for part in range(2):
            block = (part, slice(k * BLK, (k + 1) * BLK), slice(j * BLK, (j + 1) * BLK))
            top = pl.multiple_of((2 * jnp.minimum(place, cap - 1) + part) * BLK, BLK)
            both = p[block].astype(F32) + turned[pl.ds(top, BLK), :].T.astype(F32)
            out[block] = jnp.where(keep, both, jnp.zeros_like(both)).astype(BF16)


def unpack_kernel(cap, zs, kb, jb, info, pmask, *rest):
    out = rest[-1]
    wide = BLK // zs
    for s in range(zs):
        for other in range(2):
            piece = rest[2 * s + other]
            row = info[0] ^ (2 * s + other)
            for k, j, keep, place in kept(pmask, row, info[1] * jb, kb, jb):
                columns = pl.ds(pl.multiple_of((row * kb + k) * BLK, BLK), BLK)
                for part in range(2):
                    top = pl.multiple_of((2 * jnp.minimum(place, cap - 1) + part) * wide, wide)
                    here = piece[pl.ds(top, wide), :]
                    rows = slice((part * jb + j) * wide, (part * jb + j + 1) * wide)
                    out[rows, columns] = jnp.where(keep, here, jnp.zeros_like(here))


def join_kernel(zs, side, info, *rest):
    out = rest[-1]
    for i in range(2 * zs):
        out[:, pl.ds(pl.multiple_of((info[0] ^ i) * side, side), side)] = rest[i][...]


def spread_kernel(s, cap, kb, jb, info, hmask, *rest):
    packed, (dense, diagonal, slots) = rest[:-3], rest[-3:]
    row = info[0] ^ (2 * s)
    part = kb * BLK // 4
    for m in range(4):
        col = info[1] ^ m
        start = pl.multiple_of(col % 2 * (cap * BLK), BLK)
        slots[pl.ds(start, cap * BLK), :] = packed[m][: cap * BLK, :]
        start = pl.multiple_of((2 * (col % 2) + col // 2) * part, part)
        diagonal[pl.ds(start, part), :] = packed[m][cap * BLK :, :]
        if m % 2 == 0:
            continue
        left = col // 2 * (2 * jb)
        for k, j, keep, place in kept(hmask, row, left, kb, 2 * jb):
            source = pl.multiple_of(jnp.minimum(place, 2 * cap - 1) * BLK, BLK)
            start = pl.multiple_of((left + j) * BLK, BLK)
            here = slots[pl.ds(source, BLK), :]
            dense[k * BLK : (k + 1) * BLK, pl.ds(start, BLK)] = jnp.where(keep, here, jnp.zeros_like(here))
    for k in range(kb):
        rows = pl.ds(k * BLK, BLK)
        columns = pl.ds(pl.multiple_of((row * kb + k) * BLK, BLK), BLK)
        both = dense[rows, columns].astype(F32) + diagonal[k * BLK : (k + 1) * BLK, :].astype(F32)
        dense[rows, columns] = both.astype(BF16)


def integral_kernel(effective, basis, total):
    width_x, width_y = effective.shape[:2]
    for k in range(total.shape[0] // BLK):
        rows = slice(k * BLK, (k + 1) * BLK)
        for x in range(width_x):
            for y in range(width_y):
                values = basis[x, y, rows, :]
                weighted = (values.astype(F32) * effective[x, y : y + 1, :]).astype(BF16)
                here = lax.dot_general(weighted, values, (((1,), (1,)), ((), ())), preferred_element_type=F32)
                total[rows, :] = here if x + y == 0 else total[rows, :] + here


def first_kernel(joined, dense, first):
    first[...] = lax.dot_general(
        joined[...], dense[...], (((1,), (1,)), ((), ())), preferred_element_type=F32
    ).astype(BF16)


def second_kernel(slots, cap, zs, kb, jb, info, pmask, joined, *rest):
    half_square = 0.5 * TIME_STEP * TIME_STEP
    count = len(slots)
    dense, first, packed, (change, room) = rest[:count], rest[count : 2 * count], rest[2 * count : -2], rest[-2:]
    wide = BLK // zs
    for i, s in enumerate(slots):
        second = lax.dot_general(
            joined[...], dense[i][...], (((1,), (1,)), ((), ())), preferred_element_type=F32
        )
        half = second.shape[0] // 2
        real, imag = slice(0, half), slice(half, 2 * half)
        other = first[i]
        change[i, real, :] = (TIME_STEP * other[imag, :].astype(F32) - half_square * second[real, :]).astype(BF16)
        change[i, imag, :] = (-TIME_STEP * other[real, :].astype(F32) - half_square * second[imag, :]).astype(BF16)
        for k, j, _, place in kept(pmask, info[0] ^ (2 * s), info[1] * jb, kb, jb):
            for part in range(2):
                top = pl.multiple_of((2 * place + part) * wide, wide)
                rows = slice((part * jb + j) * wide, (part * jb + j + 1) * wide)
                room[i, pl.ds(top, wide), :] = change[i, rows, k * BLK : (k + 1) * BLK]
        packed[i][...] = room[i, : 2 * cap * wide, :]


def swap_row(value, bits):
    count = lax.axis_size("row")
    return lax.ppermute(value, "row", [(i, i ^ bits) for i in range(count)])


def swap_col(value, bits):
    count = lax.axis_size("col")
    return lax.ppermute(value, "col", [(i, i ^ bits) for i in range(count)])


def along(value, pairs):
    return lax.ppermute(value, "row", [(2 * a + x, 2 * b + x) for a, b in pairs for x in range(2)])


def after(done, *values):
    return lax.optimization_barrier((values, done))[0]


def effective_potential(potential):
    def beyond(axis, dim):
        count = lax.axis_size(axis)
        forward = [(i, i + 1) for i in range(count - 1)]
        backward = [(target, source) for source, target in forward]
        last = potential.shape[dim] - 1
        low = lax.ppermute(lax.slice_in_dim(potential, last, None, axis=dim), axis, forward)
        high = lax.ppermute(lax.slice_in_dim(potential, 0, 1, axis=dim), axis, backward)
        return jnp.concatenate([low, potential, high], axis=dim)

    in_x, in_y = beyond("row", 0), beyond("col", 1)
    in_z = jnp.pad(potential, ((0, 0), (0, 0), (1, 1)))
    beside = in_x[2:] + in_x[:-2]
    beside = beside + in_y[:, 2:] + in_y[:, :-2]
    beside = beside + in_z[:, :, 2:] + in_z[:, :, :-2]
    return potential + KAPPA * (beside - 6.0 * potential)


def potential_blocks(potential, basis):
    width_x, width_y, depth_z = potential.shape
    kb = basis.shape[2] // BLK
    effective = effective_potential(potential)
    (total,) = call(
        integral_kernel,
        [],
        [effective, basis],
        [shape(kb * BLK, BLK, dtype=F32)],
        flops=2 * basis.size * BLK,
        weight=32,
    )
    for bits, side in ((1, lax.axis_index("col") % 2), (2, lax.axis_index("col") // 2)):
        half = total.shape[0] // 2
        low, high = total[:half], total[half:]
        total = jnp.where(side == 0, low, high) + swap_col(jnp.where(side == 0, high, low), bits)
    factor = float(BLK * width_x * width_y * depth_z * lax.axis_size("col")) ** (-0.5)
    return (total * factor).astype(BF16)


def step(cap, cap_h, potential, basis, hamiltonian, density, hmask, pmask):
    row, col = lax.axis_index("row"), lax.axis_index("col")
    info = jnp.stack([row, col]).astype(jnp.int32)
    z = row // 2
    zs = lax.axis_size("row") // 2
    side, across = hamiltonian.shape
    order = side * lax.axis_size("row")
    kb, jb = side // BLK, across // BLK
    wide = 2 * across // zs
    piece = shape(2 * cap * BLK // zs, BLK)

    pieces = call(
        functools.partial(turn_kernel, cap, zs, kb, jb),
        [info, pmask],
        [density],
        [piece] * zs,
        scratch=[pltpu.VMEM((2 * (kb * jb + 1) * BLK, BLK), BF16)],
    )

    mine = [pieces[s] if s == 0 else swap_row(pieces[s], 2 * s) for s in range(zs)]
    theirs = [swap_row(piece, 1) for piece in mine]
    hamiltonian_core = swap_col(hamiltonian, 1)
    (potential,) = after((hamiltonian_core, *pieces), potential)
    quarter = potential_blocks(potential, basis)
    hamiltonian, quarter = after(tuple(mine[1:]), hamiltonian, quarter)
    (own,) = call(
        functools.partial(pack_kernel, cap_h, kb, jb),
        [info, hmask],
        [hamiltonian, hamiltonian_core, quarter],
        [shape(cap_h * BLK + side // 4, BLK)],
        scratch=[pltpu.VMEM(((cap_h + 2) * BLK, BLK), BF16)],
    )

    def spread(s, near, far, near_core, far_core):
        return call(
            functools.partial(spread_kernel, s, cap_h, kb, jb),
            [info, hmask],
            [near, near_core, far, far_core],
            [shape(side, order)],
            scratch=[pltpu.VMEM((side, BLK), BF16), pltpu.VMEM((2 * cap_h * BLK, BLK), BF16)],
        )[0]

    def multiply(rows_of_g):
        return call(
            first_kernel, [], [joined, rows_of_g], [shape(wide, side)], flops=2 * side * order * wide
        )[0]

    middle, outward = [(1, 2), (2, 1)], [(1, 0), (2, 3)]
    inner = (z == 1) | (z == 2)
    beside, over, own_y = swap_row(own, 2), along(own, middle), swap_col(own, 2)

    own, beside, over, own_y = after((over, own_y), own, beside, over, own_y)
    over_beside, out_near = along(beside, middle), along(over, outward)
    beside_y, own_core, own_y_core = swap_col(beside, 2), swap_col(own, 1), swap_col(own_y, 1)
    (joined,) = call(
        functools.partial(unpack_kernel, cap, zs, kb, jb),
        [info, pmask],
        [piece for pair in zip(mine, theirs) for piece in pair],
        [shape(wide, order)],
    )

    done = (out_near, beside_y, own_core, own_y_core, joined)
    beside, over, over_beside, out_near, beside_y = after(
        done, beside, over, over_beside, out_near, beside_y
    )
    slot_2 = jnp.where(inner, over_beside, out_near)
    out_far, slot_2_y = along(over_beside, outward), swap_col(slot_2, 2)
    beside_core, beside_y_core = swap_col(beside, 1), swap_col(beside_y, 1)
    dense, first, first_x = [None] * zs, [None] * zs, [None] * zs
    dense[0] = spread(0, own, own_y, own_core, own_y_core)
    first[0] = multiply(dense[0])
    first_x[0] = swap_row(first[0], 1)
    dense[1] = spread(1, beside, beside_y, beside_core, beside_y_core)
    first[1] = multiply(dense[1])

    done = (out_far, slot_2_y, first[1], first_x[0])
    over, out_far, slot_2, slot_2_y = after(done, over, out_far, slot_2, slot_2_y)
    slot_3 = jnp.where(inner, over, out_far)
    slot_3_y = swap_col(slot_3, 2)
    slot_2_core, slot_2_y_core, slot_3_core = swap_col(slot_2, 1), swap_col(slot_2_y, 1), swap_col(slot_3, 1)
    first_x[1] = swap_row(first[1], 1)
    dense[2] = spread(2, slot_2, slot_2_y, slot_2_core, slot_2_y_core)
    first[2] = multiply(dense[2])
    first_x[2] = swap_row(first[2], 1)

    (slot_3_y,) = after((slot_3_core, first_x[1], first_x[2]), slot_3_y)
    slot_3_y_core = swap_col(slot_3_y, 1)
    dense[3] = spread(3, slot_3, slot_3_y, slot_3_core, slot_3_y_core)
    first[3] = multiply(dense[3])
    first_x[3] = swap_row(first[3], 1)
    (first_joined,) = call(
        functools.partial(join_kernel, zs, side),
        [info],
        [f for pair in zip(first, first_x) for f in pair],
        [shape(wide, order)],
    )

    result = [None] * zs
    for slots in ((3,), (2,), (1,), (0,)):
        outs = call(
            functools.partial(second_kernel, slots, cap, zs, kb, jb),
            [info, pmask],
            [first_joined, *(dense[s] for s in slots), *(first[s] for s in slots)],
            [piece] * len(slots),
            scratch=[
                pltpu.VMEM((len(slots), wide, side), BF16),
                pltpu.VMEM((len(slots), 2 * (kb * jb + 1) * BLK // zs, BLK), BF16),
            ],
            flops=2 * side * order * wide * len(slots),
            weight=1 if slots[0] else 32,
        )
        for s, out in zip(slots, outs):
            result[s] = out if s == 0 else swap_row(out, 2 * s)

    return call(
        functools.partial(return_kernel, cap, zs, kb, jb),
        [info, pmask],
        [density, *result],
        [shape(2, side, across)],
        scratch=[pltpu.VMEM((2 * cap * BLK, BLK), BF16)],
    )[0]


def shards(potential, basis, hamiltonian, density, hmask, pmask):
    side, across = hamiltonian.shape
    kb, jb = side // BLK, across // BLK

    def most(mask, width):
        return mask.reshape(mask.shape[0] // kb, kb, mask.shape[1] // width, width).sum((1, 3)).max()

    cap, cap_h = kb * jb - 2, kb * jb - 4
    arguments = (potential, basis, hamiltonian, density, hmask, pmask)
    result = step(cap, cap_h, *arguments)
    more = (most(pmask, jb) > cap) | (most(hmask, 2 * jb) > 2 * cap_h)
    return lax.while_loop(
        lambda state: state[0],
        lambda state: (jnp.array(False), step(kb * jb, kb * jb, *arguments)),
        (more, result),
    )[1]


def extended_2(block, sides, width):
    for axis, dim in sides:
        count = lax.axis_size(axis)
        forward = [(i, i + 1) for i in range(count - 1)]
        backward = [(target, source) for source, target in forward]
        low = lax.ppermute(
            lax.slice_in_dim(block, block.shape[dim] - width, None, axis=dim), axis, forward
        )
        high = lax.ppermute(lax.slice_in_dim(block, 0, width, axis=dim), axis, backward)
        block = jnp.concatenate([low, block, high], axis=dim)
    return block


def gathered(potential, basis, hamiltonian, density, hmask, pmask):
    width_x, width_y, depth_z = potential.shape
    extended = extended_2(potential, (("row", 0), ("col", 1)), 1)
    padded = jnp.pad(extended, ((0, 0), (0, 0), (1, 1)))
    beside = padded[2:, 1:-1, 1:-1] + padded[:-2, 1:-1, 1:-1]
    beside = beside + padded[1:-1, 2:, 1:-1] + padded[1:-1, :-2, 1:-1]
    beside = beside + padded[1:-1, 1:-1, 2:] + padded[1:-1, 1:-1, :-2]
    effective = potential + KAPPA * (beside - 6.0 * potential)
    blocks_here = basis.shape[2] // BLK
    weighted = (basis * effective[:, :, None, :]).astype(BF16)
    partial_blocks = jnp.einsum(
        "xykaz,xykbz->kab",
        weighted.reshape(width_x, width_y, blocks_here, BLK, depth_z),
        basis.reshape(width_x, width_y, blocks_here, BLK, depth_z),
        preferred_element_type=F32,
    )
    summed = lax.psum(partial_blocks, "col")
    factor = float(BLK * width_x * width_y * depth_z * lax.axis_size("col")) ** (-0.5)
    potential_blocks = (summed * factor).astype(BF16)
    block_total = hmask.shape[0]
    blocks_wide = block_total // lax.axis_size("col")
    row_start = lax.axis_index("row") * blocks_here
    col_start = lax.axis_index("col") * blocks_wide
    hpattern = lax.dynamic_slice(hmask, (row_start, col_start), (blocks_here, blocks_wide))
    ppattern = lax.dynamic_slice(pmask, (row_start, col_start), (blocks_here, blocks_wide))
    masked_h = (
        hamiltonian.reshape(blocks_here, BLK, blocks_wide, BLK)
        * hpattern[:, None, :, None].astype(BF16)
    ).reshape(blocks_here * BLK, blocks_wide * BLK)
    masked_p = (
        density.reshape(2, blocks_here, BLK, blocks_wide, BLK)
        * ppattern[None, :, None, :, None].astype(BF16)
    ).reshape(2, blocks_here * BLK, blocks_wide * BLK)

    def diagonal_term(operand):
        local = jnp.einsum(
            "kab,skbc->skac",
            potential_blocks,
            operand.reshape(2, blocks_here, BLK, operand.shape[2]),
            preferred_element_type=F32,
        )
        return local.reshape(2, blocks_here * BLK, operand.shape[2])

    def apply(operand):
        column_whole = lax.all_gather(operand, "row", axis=1, tiled=True)
        remote = jnp.einsum(
            "rk,skc->src",
            lax.all_gather(masked_h, "col", axis=1, tiled=True),
            column_whole,
            preferred_element_type=F32,
        )
        return remote + diagonal_term(operand)

    first = apply(masked_p)
    first_rounded = first.astype(BF16)
    second = apply(first_rounded)
    base = masked_p.astype(F32)
    half_square = 0.5 * TIME_STEP * TIME_STEP
    real_part = base[0] + TIME_STEP * first[1] - half_square * second[0]
    imag_part = base[1] - TIME_STEP * first[0] - half_square * second[1]
    stacked = jnp.stack([real_part, imag_part]).reshape(2, blocks_here, BLK, blocks_wide, BLK)
    stacked = stacked * ppattern[None, :, None, :, None].astype(F32)
    return stacked.reshape(2, blocks_here * BLK, blocks_wide * BLK).astype(BF16)


def solution(mesh):
    in_specs = (
        P("row", "col", None),
        P("row", "col", None, None),
        P("row", "col"),
        P(None, "row", "col"),
        P(),
        P(),
    )
    out_specs = P(None, "row", "col")
    body = shards if (mesh.shape["row"], mesh.shape["col"]) == (8, 4) else gathered
    return jax.shard_map(body, mesh=mesh, in_specs=in_specs, out_specs=out_specs, check_vma=False)
```

```python
import functools

import jax
import jax.numpy as jnp
from jax import lax
from jax.experimental import pallas as pl
from jax.experimental.pallas import tpu as pltpu
from jax.sharding import PartitionSpec as P

BLK = 128
KAPPA = 0.4
TIME_STEP = 0.5
BF16 = jnp.bfloat16
F32 = jnp.float32
VMEM_BYTES = 48 * 1024 * 1024

SMEM_SPEC = pl.BlockSpec(memory_space=pltpu.SMEM)
VMEM_SPEC = pl.BlockSpec(memory_space=pltpu.VMEM)
ANY_SPEC = pl.BlockSpec(memory_space=pl.ANY)


def call(body, scalars, arrays, outs, scratch=(), flops=0, weight=1, left=()):
    moved = sum(a.size * a.dtype.itemsize for a in (*arrays, *left))
    moved += sum(o.size * o.dtype.itemsize for o in outs)
    return pl.pallas_call(
        body,
        out_shape=tuple(outs),
        in_specs=[SMEM_SPEC] * len(scalars) + [VMEM_SPEC] * len(arrays) + [ANY_SPEC] * len(left),
        out_specs=tuple(VMEM_SPEC for _ in outs),
        scratch_shapes=list(scratch),
        compiler_params=pltpu.CompilerParams(vmem_limit_bytes=VMEM_BYTES),
        cost_estimate=pl.CostEstimate(flops=flops, bytes_accessed=weight * moved, transcendentals=0),
    )(*scalars, *arrays, *left)


def shape(*dims, dtype=BF16):
    return jax.ShapeDtypeStruct(dims, dtype)


def kept(mask, row, start, kb, width):
    place = jnp.int32(0)
    for k in range(kb):
        for j in range(width):
            keep = mask[row * kb + k, start + j] != 0
            yield k, j, keep, place
            place = place + keep.astype(jnp.int32)


def pack_kernel(cap, kb, jb, info, hmask, h, h_core, quarter, packed, slots):
    core = info[1] % 2
    for k, j, _, place in kept(hmask, info[0], (info[1] - core) * jb, kb, 2 * jb):
        columns = slice(j % jb * BLK, (j % jb + 1) * BLK)
        block = jnp.where(core == j // jb, h[k * BLK : (k + 1) * BLK, columns], h_core[k * BLK : (k + 1) * BLK, columns])
        here = jnp.clip(place - core * cap, -1, cap) + 1
        slots[pl.ds(pl.multiple_of(here * BLK, BLK), BLK), :] = block
    packed[: cap * BLK, :] = slots[BLK : (cap + 1) * BLK, :]
    packed[cap * BLK :, :] = quarter[...]


def turn_kernel(cap, zs, kb, jb, info, pmask, p, *rest):
    pieces, turned = rest[:-1], rest[-1]
    wide = BLK // zs
    for k, j, _, place in kept(pmask, info[0], info[1] * jb, kb, jb):
        for part in range(2):
            here = p[part, k * BLK : (k + 1) * BLK, j * BLK : (j + 1) * BLK]
            top = pl.multiple_of((2 * place + part) * BLK, BLK)
            turned[pl.ds(top, BLK), :] = here.T
    for s in range(zs):
        start = pl.multiple_of(((info[0] // 2) ^ s) * wide, wide)
        for i in range(2 * cap):
            pieces[s][i * wide : (i + 1) * wide, :] = turned[pl.ds(i * BLK + start, wide), :]


def return_kernel(cap, zs, kb, jb, info, pmask, p, *rest):
    pieces, out, turned = rest[:zs], rest[zs], rest[zs + 1]
    wide = BLK // zs
    for s in range(zs):
        start = pl.multiple_of(((info[0] // 2) ^ s) * wide, wide)
        for i in range(2 * cap):
            turned[pl.ds(i * BLK + start, wide), :] = pieces[s][i * wide : (i + 1) * wide, :]
    for k, j, keep, place in kept(pmask, info[0], info[1] * jb, kb, jb):
        for part in range(2):
            block = (part, slice(k * BLK, (k + 1) * BLK), slice(j * BLK, (j + 1) * BLK))
            top = pl.multiple_of((2 * jnp.minimum(place, cap - 1) + part) * BLK, BLK)
            both = p[block].astype(F32) + turned[pl.ds(top, BLK), :].T.astype(F32)
            out[block] = jnp.where(keep, both, jnp.zeros_like(both)).astype(BF16)


def unpack_kernel(cap, zs, kb, jb, info, pmask, *rest):
    out = rest[-1]
    wide = BLK // zs
    for s in range(zs):
        for other in range(2):
            piece, base = (rest[zs], s * 2 * cap * wide) if other else (rest[s], 0)
            row = info[0] ^ (2 * s + other)
            for k, j, keep, place in kept(pmask, row, info[1] * jb, kb, jb):
                columns = pl.ds(pl.multiple_of((row * kb + k) * BLK, BLK), BLK)
                for part in range(2):
                    top = pl.multiple_of(base + (2 * jnp.minimum(place, cap - 1) + part) * wide, wide)
                    here = piece[pl.ds(top, wide), :]
                    rows = slice((part * jb + j) * wide, (part * jb + j + 1) * wide)
                    out[rows, columns] = jnp.where(keep, here, jnp.zeros_like(here))


def spread_kernel(s, cap, kb, jb, info, hmask, *rest):
    (near, far, core), (dense, diagonal, slots) = rest[:-3], rest[-3:]
    size = cap * BLK + kb * BLK // 4
    row = info[0] ^ (2 * s)
    part = kb * BLK // 4
    for m in range(4):
        col = info[1] ^ m
        start = pl.multiple_of(col % 2 * (cap * BLK), BLK)
        packed, base = ((near, 0), (core, 0), (far, 0), (core, size))[m]
        slots[pl.ds(start, cap * BLK), :] = packed[base : base + cap * BLK, :]
        start = pl.multiple_of((2 * (col % 2) + col // 2) * part, part)
        diagonal[pl.ds(start, part), :] = packed[base + cap * BLK : base + size, :]
        if m % 2 == 0:
            continue
        left = col // 2 * (2 * jb)
        for k, j, keep, place in kept(hmask, row, left, kb, 2 * jb):
            source = pl.multiple_of(jnp.minimum(place, 2 * cap - 1) * BLK, BLK)
            start = pl.multiple_of((left + j) * BLK, BLK)
            here = slots[pl.ds(source, BLK), :]
            dense[k * BLK : (k + 1) * BLK, pl.ds(start, BLK)] = jnp.where(keep, here, jnp.zeros_like(here))
    for k in range(kb):
        rows = pl.ds(k * BLK, BLK)
        columns = pl.ds(pl.multiple_of((row * kb + k) * BLK, BLK), BLK)
        both = dense[rows, columns].astype(F32) + diagonal[k * BLK : (k + 1) * BLK, :].astype(F32)
        dense[rows, columns] = both.astype(BF16)


def integral_kernel(effective, basis, total):
    width_x, width_y = effective.shape[:2]
    for k in range(total.shape[0] // BLK):
        rows = slice(k * BLK, (k + 1) * BLK)
        for x in range(width_x):
            for y in range(width_y):
                values = basis[x, y, rows, :]
                weighted = (values.astype(F32) * effective[x, y : y + 1, :]).astype(BF16)
                here = lax.dot_general(weighted, values, (((1,), (1,)), ((), ())), preferred_element_type=F32)
                total[rows, :] = here if x + y == 0 else total[rows, :] + here


def first_kernel(joined, dense, first):
    first[...] = lax.dot_general(
        joined[...], dense[...], (((1,), (1,)), ((), ())), preferred_element_type=F32
    ).astype(BF16)


def second_kernel(slots, cap, zs, kb, jb, info, pmask, *rest):
    half_square = 0.5 * TIME_STEP * TIME_STEP
    count = len(slots)
    pieces, dense, packed = rest[: 2 * zs], rest[2 * zs : 2 * zs + count], rest[2 * zs + count : -5]
    joined, held, change, room, arrived = rest[-5:]
    copies = [pltpu.make_async_copy(dense[i], held.at[i], arrived.at[i]) for i in range(count)]
    for copy in copies:
        copy.start()
    side = kb * BLK
    for i in range(2 * zs):
        joined[:, pl.ds(pl.multiple_of((info[0] ^ i) * side, side), side)] = pieces[i][...]
    wide = BLK // zs
    for i, s in enumerate(slots):
        copies[i].wait()
        second = lax.dot_general(
            joined[...], held[i], (((1,), (1,)), ((), ())), preferred_element_type=F32
        )
        half = second.shape[0] // 2
        real, imag = slice(0, half), slice(half, 2 * half)
        first = pieces[2 * s]
        change[i, real, :] = (TIME_STEP * first[imag, :].astype(F32) - half_square * second[real, :]).astype(BF16)
        change[i, imag, :] = (-TIME_STEP * first[real, :].astype(F32) - half_square * second[imag, :]).astype(BF16)
        for k, j, _, place in kept(pmask, info[0] ^ (2 * s), info[1] * jb, kb, jb):
            for part in range(2):
                top = pl.multiple_of((2 * place + part) * wide, wide)
                rows = slice((part * jb + j) * wide, (part * jb + j + 1) * wide)
                room[i, pl.ds(top, wide), :] = change[i, rows, k * BLK : (k + 1) * BLK]
        packed[i][...] = room[i, : 2 * cap * wide, :]


def swap_row(value, bits):
    count = lax.axis_size("row")
    return lax.ppermute(value, "row", [(i, i ^ bits) for i in range(count)])


def swap_col(value, bits):
    count = lax.axis_size("col")
    return lax.ppermute(value, "col", [(i, i ^ bits) for i in range(count)])


def along(value, pairs):
    return lax.ppermute(value, "row", [(2 * a + x, 2 * b + x) for a, b in pairs for x in range(2)])


def after(done, *values):
    return lax.optimization_barrier((values, done))[0]


def effective_potential(potential):
    def beyond(axis, dim):
        count = lax.axis_size(axis)
        forward = [(i, i + 1) for i in range(count - 1)]
        backward = [(target, source) for source, target in forward]
        last = potential.shape[dim] - 1
        low = lax.ppermute(lax.slice_in_dim(potential, last, None, axis=dim), axis, forward)
        high = lax.ppermute(lax.slice_in_dim(potential, 0, 1, axis=dim), axis, backward)
        return jnp.concatenate([low, potential, high], axis=dim)

    in_x, in_y = beyond("row", 0), beyond("col", 1)
    in_z = jnp.pad(potential, ((0, 0), (0, 0), (1, 1)))
    beside = in_x[2:] + in_x[:-2]
    beside = beside + in_y[:, 2:] + in_y[:, :-2]
    beside = beside + in_z[:, :, 2:] + in_z[:, :, :-2]
    return potential + KAPPA * (beside - 6.0 * potential)


def potential_blocks(potential, basis, gate):
    width_x, width_y, depth_z = potential.shape
    kb = basis.shape[2] // BLK
    effective = effective_potential(potential)
    (total,) = call(
        integral_kernel,
        [],
        [effective, basis],
        [shape(kb * BLK, BLK, dtype=F32)],
        flops=2 * basis.size * BLK,
        weight=32,
    )
    (total,) = after(gate, total)
    part = total.shape[0] // 4

    def of(col):
        return lax.dynamic_slice_in_dim(total, (2 * (col % 2) + col // 2) * part, part, axis=0)

    col = lax.axis_index("col")
    total = of(col) + swap_col(of(col ^ 1), 1) + swap_col(of(col ^ 2), 2) + swap_col(of(col ^ 3), 3)
    factor = float(BLK * width_x * width_y * depth_z * lax.axis_size("col")) ** (-0.5)
    return (total * factor).astype(BF16)


def step(cap, cap_h, potential, basis, hamiltonian, density, hmask, pmask):
    row, col = lax.axis_index("row"), lax.axis_index("col")
    info = jnp.stack([row, col]).astype(jnp.int32)
    z = row // 2
    zs = lax.axis_size("row") // 2
    side, across = hamiltonian.shape
    order = side * lax.axis_size("row")
    kb, jb = side // BLK, across // BLK
    wide = 2 * across // zs
    piece = shape(2 * cap * BLK // zs, BLK)

    pieces = call(
        functools.partial(turn_kernel, cap, zs, kb, jb),
        [info, pmask],
        [density],
        [piece] * zs,
        scratch=[pltpu.VMEM((2 * (kb * jb + 1) * BLK, BLK), BF16)],
    )

    mine = [pieces[s] if s == 0 else swap_row(pieces[s], 2 * s) for s in range(zs)]
    theirs = swap_row(jnp.concatenate(mine), 1)
    hamiltonian_core = swap_col(hamiltonian, 1)
    quarter = potential_blocks(potential, basis, (mine[1], mine[2], mine[3]))
    (own,) = call(
        functools.partial(pack_kernel, cap_h, kb, jb),
        [info, hmask],
        [hamiltonian, hamiltonian_core, quarter],
        [shape(cap_h * BLK + side // 4, BLK)],
        scratch=[pltpu.VMEM(((cap_h + 2) * BLK, BLK), BF16)],
    )

    def spread(s, near, far, core):
        return call(
            functools.partial(spread_kernel, s, cap_h, kb, jb),
            [info, hmask],
            [near, far, core],
            [shape(side, order)],
            scratch=[pltpu.VMEM((side, BLK), BF16), pltpu.VMEM((2 * cap_h * BLK, BLK), BF16)],
        )[0]

    def multiply(rows_of_g):
        return call(
            first_kernel, [], [joined, rows_of_g], [shape(wide, side)], flops=2 * side * order * wide
        )[0]

    middle, outward = [(1, 2), (2, 1)], [(1, 0), (2, 3)]
    inner = (z == 1) | (z == 2)
    beside, over, own_y = swap_row(own, 2), along(own, middle), swap_col(own, 2)

    def other_core(near, far):
        return swap_col(jnp.concatenate([near, far]), 1)

    own, beside, over, own_y = after((over, own_y), own, beside, over, own_y)
    over_beside, out_near, beside_y = along(beside, middle), along(over, outward), swap_col(beside, 2)
    own_core = other_core(own, own_y)
    (joined,) = call(
        functools.partial(unpack_kernel, cap, zs, kb, jb),
        [info, pmask],
        [*mine, theirs],
        [shape(wide, order)],
    )

    done = (out_near, beside_y, own_core, joined)
    beside, over, over_beside, out_near, beside_y = after(
        done, beside, over, over_beside, out_near, beside_y
    )
    slot_2 = jnp.where(inner, over_beside, out_near)
    out_far, slot_2_y, beside_core = along(over_beside, outward), swap_col(slot_2, 2), other_core(beside, beside_y)
    dense, first, first_x = [None] * zs, [None] * zs, [None] * zs
    dense[0] = spread(0, own, own_y, own_core)
    first[0] = multiply(dense[0])
    first_x[0] = swap_row(first[0], 1)
    dense[1] = spread(1, beside, beside_y, beside_core)
    first[1] = multiply(dense[1])

    done = (out_far, slot_2_y, first[1], first_x[0])
    over, out_far, slot_2, slot_2_y = after(done, over, out_far, slot_2, slot_2_y)
    slot_3 = jnp.where(inner, over, out_far)
    slot_3_y, slot_2_core = swap_col(slot_3, 2), other_core(slot_2, slot_2_y)
    first_x[1] = swap_row(first[1], 1)
    dense[2] = spread(2, slot_2, slot_2_y, slot_2_core)
    first[2] = multiply(dense[2])
    first_x[2] = swap_row(first[2], 1)

    (slot_3_y,) = after((first_x[1], first[2]), slot_3_y)
    slot_3_core = other_core(slot_3, slot_3_y)
    dense[3] = spread(3, slot_3, slot_3_y, slot_3_core)
    first[3] = multiply(dense[3])
    first_x[3] = swap_row(first[3], 1)
    everything = [f for pair in zip(first, first_x) for f in pair]
    result = [None] * zs
    for slots in ((3, 2, 1), (0,)):
        count = len(slots)
        outs = call(
            functools.partial(second_kernel, slots, cap, zs, kb, jb),
            [info, pmask],
            everything,
            [piece] * count,
            scratch=[
                pltpu.VMEM((wide, order), BF16),
                pltpu.VMEM((count, side, order), BF16),
                pltpu.VMEM((count, wide, side), BF16),
                pltpu.VMEM((count, 2 * (kb * jb + 1) * BLK // zs, BLK), BF16),
                pltpu.SemaphoreType.DMA((count,)),
            ],
            flops=2 * side * order * wide * count,
            left=[dense[s] for s in slots],
        )
        for s, out in zip(slots, outs):
            result[s] = out if s == 0 else swap_row(out, 2 * s)

    return call(
        functools.partial(return_kernel, cap, zs, kb, jb),
        [info, pmask],
        [density, *result],
        [shape(2, side, across)],
        scratch=[pltpu.VMEM((2 * cap * BLK, BLK), BF16)],
    )[0]


def shards(potential, basis, hamiltonian, density, hmask, pmask):
    side, across = hamiltonian.shape
    kb, jb = side // BLK, across // BLK

    def most(mask, width):
        return mask.reshape(mask.shape[0] // kb, kb, mask.shape[1] // width, width).sum((1, 3)).max()

    cap, cap_h = kb * jb - 2, kb * jb - 4
    arguments = (potential, basis, hamiltonian, density, hmask, pmask)
    result = step(cap, cap_h, *arguments)
    more = (most(pmask, jb) > cap) | (most(hmask, 2 * jb) > 2 * cap_h)
    return lax.while_loop(
        lambda state: state[0],
        lambda state: (jnp.array(False), step(kb * jb, kb * jb, *arguments)),
        (more, result),
    )[1]


def extended_2(block, sides, width):
    for axis, dim in sides:
        count = lax.axis_size(axis)
        forward = [(i, i + 1) for i in range(count - 1)]
        backward = [(target, source) for source, target in forward]
        low = lax.ppermute(
            lax.slice_in_dim(block, block.shape[dim] - width, None, axis=dim), axis, forward
        )
        high = lax.ppermute(lax.slice_in_dim(block, 0, width, axis=dim), axis, backward)
        block = jnp.concatenate([low, block, high], axis=dim)
    return block


def gathered(potential, basis, hamiltonian, density, hmask, pmask):
    width_x, width_y, depth_z = potential.shape
    extended = extended_2(potential, (("row", 0), ("col", 1)), 1)
    padded = jnp.pad(extended, ((0, 0), (0, 0), (1, 1)))
    beside = padded[2:, 1:-1, 1:-1] + padded[:-2, 1:-1, 1:-1]
    beside = beside + padded[1:-1, 2:, 1:-1] + padded[1:-1, :-2, 1:-1]
    beside = beside + padded[1:-1, 1:-1, 2:] + padded[1:-1, 1:-1, :-2]
    effective = potential + KAPPA * (beside - 6.0 * potential)
    blocks_here = basis.shape[2] // BLK
    weighted = (basis * effective[:, :, None, :]).astype(BF16)
    partial_blocks = jnp.einsum(
        "xykaz,xykbz->kab",
        weighted.reshape(width_x, width_y, blocks_here, BLK, depth_z),
        basis.reshape(width_x, width_y, blocks_here, BLK, depth_z),
        preferred_element_type=F32,
    )
    summed = lax.psum(partial_blocks, "col")
    factor = float(BLK * width_x * width_y * depth_z * lax.axis_size("col")) ** (-0.5)
    potential_blocks = (summed * factor).astype(BF16)
    block_total = hmask.shape[0]
    blocks_wide = block_total // lax.axis_size("col")
    row_start = lax.axis_index("row") * blocks_here
    col_start = lax.axis_index("col") * blocks_wide
    hpattern = lax.dynamic_slice(hmask, (row_start, col_start), (blocks_here, blocks_wide))
    ppattern = lax.dynamic_slice(pmask, (row_start, col_start), (blocks_here, blocks_wide))
    masked_h = (
        hamiltonian.reshape(blocks_here, BLK, blocks_wide, BLK)
        * hpattern[:, None, :, None].astype(BF16)
    ).reshape(blocks_here * BLK, blocks_wide * BLK)
    masked_p = (
        density.reshape(2, blocks_here, BLK, blocks_wide, BLK)
        * ppattern[None, :, None, :, None].astype(BF16)
    ).reshape(2, blocks_here * BLK, blocks_wide * BLK)

    def diagonal_term(operand):
        local = jnp.einsum(
            "kab,skbc->skac",
            potential_blocks,
            operand.reshape(2, blocks_here, BLK, operand.shape[2]),
            preferred_element_type=F32,
        )
        return local.reshape(2, blocks_here * BLK, operand.shape[2])

    def apply(operand):
        column_whole = lax.all_gather(operand, "row", axis=1, tiled=True)
        remote = jnp.einsum(
            "rk,skc->src",
            lax.all_gather(masked_h, "col", axis=1, tiled=True),
            column_whole,
            preferred_element_type=F32,
        )
        return remote + diagonal_term(operand)

    first = apply(masked_p)
    first_rounded = first.astype(BF16)
    second = apply(first_rounded)
    base = masked_p.astype(F32)
    half_square = 0.5 * TIME_STEP * TIME_STEP
    real_part = base[0] + TIME_STEP * first[1] - half_square * second[0]
    imag_part = base[1] - TIME_STEP * first[0] - half_square * second[1]
    stacked = jnp.stack([real_part, imag_part]).reshape(2, blocks_here, BLK, blocks_wide, BLK)
    stacked = stacked * ppattern[None, :, None, :, None].astype(F32)
    return stacked.reshape(2, blocks_here * BLK, blocks_wide * BLK).astype(BF16)


def solution(mesh):
    in_specs = (
        P("row", "col", None),
        P("row", "col", None, None),
        P("row", "col"),
        P(None, "row", "col"),
        P(),
        P(),
    )
    out_specs = P(None, "row", "col")
    body = shards if (mesh.shape["row"], mesh.shape["col"]) == (8, 4) else gathered
    return jax.shard_map(body, mesh=mesh, in_specs=in_specs, out_specs=out_specs, check_vma=False)
```

```python
import functools

import jax
import jax.numpy as jnp
from jax import lax
from jax.experimental import pallas as pl
from jax.experimental.pallas import tpu as pltpu
from jax.sharding import PartitionSpec as P

BLK = 128
KAPPA = 0.4
TIME_STEP = 0.5
BF16 = jnp.bfloat16
F32 = jnp.float32
VMEM_BYTES = 48 * 1024 * 1024

SMEM_SPEC = pl.BlockSpec(memory_space=pltpu.SMEM)
VMEM_SPEC = pl.BlockSpec(memory_space=pltpu.VMEM)


def call(body, scalars, arrays, outs, scratch=(), flops=0, weight=1):
    moved = sum(a.size * a.dtype.itemsize for a in arrays)
    moved += sum(o.size * o.dtype.itemsize for o in outs)
    return pl.pallas_call(
        body,
        out_shape=tuple(outs),
        in_specs=[SMEM_SPEC] * len(scalars) + [VMEM_SPEC] * len(arrays),
        out_specs=tuple(VMEM_SPEC for _ in outs),
        scratch_shapes=list(scratch),
        compiler_params=pltpu.CompilerParams(vmem_limit_bytes=VMEM_BYTES),
        cost_estimate=pl.CostEstimate(flops=flops, bytes_accessed=weight * moved, transcendentals=0),
    )(*scalars, *arrays)


def shape(*dims, dtype=BF16):
    return jax.ShapeDtypeStruct(dims, dtype)


def kept(mask, row, start, kb, width):
    place = jnp.int32(0)
    for k in range(kb):
        for j in range(width):
            keep = mask[row * kb + k, start + j] != 0
            yield k, j, keep, place
            place = place + keep.astype(jnp.int32)


def pack_kernel(cap, kb, jb, info, hmask, h, h_core, quarter, packed, slots):
    core = info[1] % 2
    for k, j, _, place in kept(hmask, info[0], (info[1] - core) * jb, kb, 2 * jb):
        columns = slice(j % jb * BLK, (j % jb + 1) * BLK)
        block = jnp.where(core == j // jb, h[k * BLK : (k + 1) * BLK, columns], h_core[k * BLK : (k + 1) * BLK, columns])
        here = jnp.clip(place - core * cap, -1, cap) + 1
        slots[pl.ds(pl.multiple_of(here * BLK, BLK), BLK), :] = block
    packed[: cap * BLK, :] = slots[BLK : (cap + 1) * BLK, :]
    packed[cap * BLK :, :] = quarter[...]


def turn_kernel(cap, zs, kb, jb, info, pmask, p, *rest):
    pieces, turned = rest[:-1], rest[-1]
    wide = BLK // zs
    for k, j, _, place in kept(pmask, info[0], info[1] * jb, kb, jb):
        for part in range(2):
            here = p[part, k * BLK : (k + 1) * BLK, j * BLK : (j + 1) * BLK]
            top = pl.multiple_of((2 * place + part) * BLK, BLK)
            turned[pl.ds(top, BLK), :] = here.T
    for s in range(zs):
        start = pl.multiple_of(((info[0] // 2) ^ s) * wide, wide)
        for i in range(2 * cap):
            pieces[s][i * wide : (i + 1) * wide, :] = turned[pl.ds(i * BLK + start, wide), :]


def return_kernel(cap, zs, kb, jb, info, pmask, p, *rest):
    pieces, out, turned = rest[:zs], rest[zs], rest[zs + 1]
    wide = BLK // zs
    for s in range(zs):
        start = pl.multiple_of(((info[0] // 2) ^ s) * wide, wide)
        for i in range(2 * cap):
            turned[pl.ds(i * BLK + start, wide), :] = pieces[s][i * wide : (i + 1) * wide, :]
    for k, j, keep, place in kept(pmask, info[0], info[1] * jb, kb, jb):
        for part in range(2):
            block = (part, slice(k * BLK, (k + 1) * BLK), slice(j * BLK, (j + 1) * BLK))
            top = pl.multiple_of((2 * jnp.minimum(place, cap - 1) + part) * BLK, BLK)
            both = p[block].astype(F32) + turned[pl.ds(top, BLK), :].T.astype(F32)
            out[block] = jnp.where(keep, both, jnp.zeros_like(both)).astype(BF16)


def unpack_kernel(cap, zs, kb, jb, info, pmask, *rest):
    out = rest[-1]
    wide = BLK // zs
    for s in range(zs):
        for other in range(2):
            piece, base = (rest[zs], s * 2 * cap * wide) if other else (rest[s], 0)
            row = info[0] ^ (2 * s + other)
            for k, j, keep, place in kept(pmask, row, info[1] * jb, kb, jb):
                columns = pl.ds(pl.multiple_of((row * kb + k) * BLK, BLK), BLK)
                for part in range(2):
                    top = pl.multiple_of(base + (2 * jnp.minimum(place, cap - 1) + part) * wide, wide)
                    here = piece[pl.ds(top, wide), :]
                    rows = slice((part * jb + j) * wide, (part * jb + j + 1) * wide)
                    out[rows, columns] = jnp.where(keep, here, jnp.zeros_like(here))


def join_kernel(zs, side, info, *rest):
    out = rest[-1]
    for i in range(2 * zs):
        out[:, pl.ds(pl.multiple_of((info[0] ^ i) * side, side), side)] = rest[i][...]


def spread_kernel(s, cap, kb, jb, info, hmask, *rest):
    (near, far, core), (dense, diagonal, slots) = rest[:-3], rest[-3:]
    size = cap * BLK + kb * BLK // 4
    row = info[0] ^ (2 * s)
    part = kb * BLK // 4
    for m in range(4):
        col = info[1] ^ m
        start = pl.multiple_of(col % 2 * (cap * BLK), BLK)
        packed, base = ((near, 0), (core, 0), (far, 0), (core, size))[m]
        slots[pl.ds(start, cap * BLK), :] = packed[base : base + cap * BLK, :]
        start = pl.multiple_of((2 * (col % 2) + col // 2) * part, part)
        diagonal[pl.ds(start, part), :] = packed[base + cap * BLK : base + size, :]
        if m % 2 == 0:
            continue
        left = col // 2 * (2 * jb)
        for k, j, keep, place in kept(hmask, row, left, kb, 2 * jb):
            source = pl.multiple_of(jnp.minimum(place, 2 * cap - 1) * BLK, BLK)
            start = pl.multiple_of((left + j) * BLK, BLK)
            here = slots[pl.ds(source, BLK), :]
            dense[k * BLK : (k + 1) * BLK, pl.ds(start, BLK)] = jnp.where(keep, here, jnp.zeros_like(here))
    for k in range(kb):
        rows = pl.ds(k * BLK, BLK)
        columns = pl.ds(pl.multiple_of((row * kb + k) * BLK, BLK), BLK)
        both = dense[rows, columns].astype(F32) + diagonal[k * BLK : (k + 1) * BLK, :].astype(F32)
        dense[rows, columns] = both.astype(BF16)


def integral_kernel(effective, basis, total):
    width_x, width_y = effective.shape[:2]
    for k in range(total.shape[0] // BLK):
        rows = slice(k * BLK, (k + 1) * BLK)
        for x in range(width_x):
            for y in range(width_y):
                values = basis[x, y, rows, :]
                weighted = (values.astype(F32) * effective[x, y : y + 1, :]).astype(BF16)
                here = lax.dot_general(weighted, values, (((1,), (1,)), ((), ())), preferred_element_type=F32)
                total[rows, :] = here if x + y == 0 else total[rows, :] + here


def first_kernel(joined, dense, first):
    first[...] = lax.dot_general(
        joined[...], dense[...], (((1,), (1,)), ((), ())), preferred_element_type=F32
    ).astype(BF16)


def second_kernel(slots, cap, zs, kb, jb, info, pmask, joined, *rest):
    half_square = 0.5 * TIME_STEP * TIME_STEP
    count = len(slots)
    dense, first, packed, (change, room) = rest[:count], rest[count : 2 * count], rest[2 * count : -2], rest[-2:]
    wide = BLK // zs
    for i, s in enumerate(slots):
        second = lax.dot_general(
            joined[...], dense[i][...], (((1,), (1,)), ((), ())), preferred_element_type=F32
        )
        half = second.shape[0] // 2
        real, imag = slice(0, half), slice(half, 2 * half)
        other = first[i]
        change[i, real, :] = (TIME_STEP * other[imag, :].astype(F32) - half_square * second[real, :]).astype(BF16)
        change[i, imag, :] = (-TIME_STEP * other[real, :].astype(F32) - half_square * second[imag, :]).astype(BF16)
        for k, j, _, place in kept(pmask, info[0] ^ (2 * s), info[1] * jb, kb, jb):
            for part in range(2):
                top = pl.multiple_of((2 * place + part) * wide, wide)
                rows = slice((part * jb + j) * wide, (part * jb + j + 1) * wide)
                room[i, pl.ds(top, wide), :] = change[i, rows, k * BLK : (k + 1) * BLK]
        packed[i][...] = room[i, : 2 * cap * wide, :]


def swap_row(value, bits):
    count = lax.axis_size("row")
    return lax.ppermute(value, "row", [(i, i ^ bits) for i in range(count)])


def swap_col(value, bits):
    count = lax.axis_size("col")
    return lax.ppermute(value, "col", [(i, i ^ bits) for i in range(count)])


def along(value, pairs):
    return lax.ppermute(value, "row", [(2 * a + x, 2 * b + x) for a, b in pairs for x in range(2)])


def after(done, *values):
    return lax.optimization_barrier((values, done))[0]


def effective_potential(potential):
    def beyond(axis, dim):
        count = lax.axis_size(axis)
        forward = [(i, i + 1) for i in range(count - 1)]
        backward = [(target, source) for source, target in forward]
        last = potential.shape[dim] - 1
        low = lax.ppermute(lax.slice_in_dim(potential, last, None, axis=dim), axis, forward)
        high = lax.ppermute(lax.slice_in_dim(potential, 0, 1, axis=dim), axis, backward)
        return jnp.concatenate([low, potential, high], axis=dim)

    in_x, in_y = beyond("row", 0), beyond("col", 1)
    in_z = jnp.pad(potential, ((0, 0), (0, 0), (1, 1)))
    beside = in_x[2:] + in_x[:-2]
    beside = beside + in_y[:, 2:] + in_y[:, :-2]
    beside = beside + in_z[:, :, 2:] + in_z[:, :, :-2]
    return potential + KAPPA * (beside - 6.0 * potential)


def potential_blocks(potential, basis, gate):
    width_x, width_y, depth_z = potential.shape
    kb = basis.shape[2] // BLK
    effective = effective_potential(potential)
    (total,) = call(
        integral_kernel,
        [],
        [effective, basis],
        [shape(kb * BLK, BLK, dtype=F32)],
        flops=2 * basis.size * BLK,
        weight=32,
    )
    (total,) = after(gate, total)
    part = total.shape[0] // 4

    def of(col):
        return lax.dynamic_slice_in_dim(total, (2 * (col % 2) + col // 2) * part, part, axis=0)

    col = lax.axis_index("col")
    total = of(col) + swap_col(of(col ^ 1), 1) + swap_col(of(col ^ 2), 2) + swap_col(of(col ^ 3), 3)
    factor = float(BLK * width_x * width_y * depth_z * lax.axis_size("col")) ** (-0.5)
    return (total * factor).astype(BF16)


def step(cap, cap_h, potential, basis, hamiltonian, density, hmask, pmask):
    row, col = lax.axis_index("row"), lax.axis_index("col")
    info = jnp.stack([row, col]).astype(jnp.int32)
    z = row // 2
    zs = lax.axis_size("row") // 2
    side, across = hamiltonian.shape
    order = side * lax.axis_size("row")
    kb, jb = side // BLK, across // BLK
    wide = 2 * across // zs
    piece = shape(2 * cap * BLK // zs, BLK)

    pieces = call(
        functools.partial(turn_kernel, cap, zs, kb, jb),
        [info, pmask],
        [density],
        [piece] * zs,
        scratch=[pltpu.VMEM((2 * (kb * jb + 1) * BLK, BLK), BF16)],
    )

    mine = [pieces[s] if s == 0 else swap_row(pieces[s], 2 * s) for s in range(zs)]
    theirs = swap_row(jnp.concatenate(mine), 1)
    hamiltonian_core = swap_col(hamiltonian, 1)
    quarter = potential_blocks(potential, basis, (mine[1], mine[2], mine[3]))
    (own,) = call(
        functools.partial(pack_kernel, cap_h, kb, jb),
        [info, hmask],
        [hamiltonian, hamiltonian_core, quarter],
        [shape(cap_h * BLK + side // 4, BLK)],
        scratch=[pltpu.VMEM(((cap_h + 2) * BLK, BLK), BF16)],
    )

    def spread(s, near, far, core):
        return call(
            functools.partial(spread_kernel, s, cap_h, kb, jb),
            [info, hmask],
            [near, far, core],
            [shape(side, order)],
            scratch=[pltpu.VMEM((side, BLK), BF16), pltpu.VMEM((2 * cap_h * BLK, BLK), BF16)],
        )[0]

    def multiply(rows_of_g):
        return call(
            first_kernel, [], [joined, rows_of_g], [shape(wide, side)], flops=2 * side * order * wide
        )[0]

    middle, outward = [(1, 2), (2, 1)], [(1, 0), (2, 3)]
    inner = (z == 1) | (z == 2)
    beside, over, own_y = swap_row(own, 2), along(own, middle), swap_col(own, 2)

    def other_core(near, far):
        return swap_col(jnp.concatenate([near, far]), 1)

    own, beside, over, own_y = after((over, own_y), own, beside, over, own_y)
    over_beside, out_near, beside_y = along(beside, middle), along(over, outward), swap_col(beside, 2)
    own_core = other_core(own, own_y)
    (joined,) = call(
        functools.partial(unpack_kernel, cap, zs, kb, jb),
        [info, pmask],
        [*mine, theirs],
        [shape(wide, order)],
    )

    dense, first, first_x = [None] * zs, [None] * zs, [None] * zs
    dense[0] = spread(0, own, own_y, own_core)
    first[0] = multiply(dense[0])

    done = (out_near, beside_y, first[0])
    beside, over, over_beside, out_near, beside_y = after(
        done, beside, over, over_beside, out_near, beside_y
    )
    slot_2 = jnp.where(inner, over_beside, out_near)
    out_far, slot_2_y, beside_core = along(over_beside, outward), swap_col(slot_2, 2), other_core(beside, beside_y)
    first_x[0] = swap_row(first[0], 1)
    dense[1] = spread(1, beside, beside_y, beside_core)
    first[1] = multiply(dense[1])

    done = (out_far, slot_2_y, first[1], first_x[0])
    over, out_far, slot_2, slot_2_y = after(done, over, out_far, slot_2, slot_2_y)
    slot_3 = jnp.where(inner, over, out_far)
    slot_3_y, slot_2_core = swap_col(slot_3, 2), other_core(slot_2, slot_2_y)
    first_x[1] = swap_row(first[1], 1)
    dense[2] = spread(2, slot_2, slot_2_y, slot_2_core)
    first[2] = multiply(dense[2])
    first_x[2] = swap_row(first[2], 1)

    (slot_3_y,) = after((first_x[1], first[2]), slot_3_y)
    slot_3_core = other_core(slot_3, slot_3_y)
    dense[3] = spread(3, slot_3, slot_3_y, slot_3_core)
    first[3] = multiply(dense[3])
    first_x[3] = swap_row(first[3], 1)
    (first_joined,) = call(
        functools.partial(join_kernel, zs, side),
        [info],
        [f for pair in zip(first, first_x) for f in pair],
        [shape(wide, order)],
    )

    result = [None] * zs
    for slots in ((3,), (2,), (1,), (0,)):
        outs = call(
            functools.partial(second_kernel, slots, cap, zs, kb, jb),
            [info, pmask],
            [first_joined, *(dense[s] for s in slots), *(first[s] for s in slots)],
            [piece] * len(slots),
            scratch=[
                pltpu.VMEM((len(slots), wide, side), BF16),
                pltpu.VMEM((len(slots), 2 * (kb * jb + 1) * BLK // zs, BLK), BF16),
            ],
            flops=2 * side * order * wide * len(slots),
        )
        for s, out in zip(slots, outs):
            result[s] = out if s == 0 else swap_row(out, 2 * s)

    return call(
        functools.partial(return_kernel, cap, zs, kb, jb),
        [info, pmask],
        [density, *result],
        [shape(2, side, across)],
        scratch=[pltpu.VMEM((2 * cap * BLK, BLK), BF16)],
    )[0]


def shards(potential, basis, hamiltonian, density, hmask, pmask):
    side, across = hamiltonian.shape
    kb, jb = side // BLK, across // BLK

    def most(mask, width):
        return mask.reshape(mask.shape[0] // kb, kb, mask.shape[1] // width, width).sum((1, 3)).max()

    cap, cap_h = kb * jb - 2, kb * jb - 4
    arguments = (potential, basis, hamiltonian, density, hmask, pmask)
    result = step(cap, cap_h, *arguments)
    more = (most(pmask, jb) > cap) | (most(hmask, 2 * jb) > 2 * cap_h)
    return lax.while_loop(
        lambda state: state[0],
        lambda state: (jnp.array(False), step(kb * jb, kb * jb, *arguments)),
        (more, result),
    )[1]


def extended_2(block, sides, width):
    for axis, dim in sides:
        count = lax.axis_size(axis)
        forward = [(i, i + 1) for i in range(count - 1)]
        backward = [(target, source) for source, target in forward]
        low = lax.ppermute(
            lax.slice_in_dim(block, block.shape[dim] - width, None, axis=dim), axis, forward
        )
        high = lax.ppermute(lax.slice_in_dim(block, 0, width, axis=dim), axis, backward)
        block = jnp.concatenate([low, block, high], axis=dim)
    return block


def gathered(potential, basis, hamiltonian, density, hmask, pmask):
    width_x, width_y, depth_z = potential.shape
    extended = extended_2(potential, (("row", 0), ("col", 1)), 1)
    padded = jnp.pad(extended, ((0, 0), (0, 0), (1, 1)))
    beside = padded[2:, 1:-1, 1:-1] + padded[:-2, 1:-1, 1:-1]
    beside = beside + padded[1:-1, 2:, 1:-1] + padded[1:-1, :-2, 1:-1]
    beside = beside + padded[1:-1, 1:-1, 2:] + padded[1:-1, 1:-1, :-2]
    effective = potential + KAPPA * (beside - 6.0 * potential)
    blocks_here = basis.shape[2] // BLK
    weighted = (basis * effective[:, :, None, :]).astype(BF16)
    partial_blocks = jnp.einsum(
        "xykaz,xykbz->kab",
        weighted.reshape(width_x, width_y, blocks_here, BLK, depth_z),
        basis.reshape(width_x, width_y, blocks_here, BLK, depth_z),
        preferred_element_type=F32,
    )
    summed = lax.psum(partial_blocks, "col")
    factor = float(BLK * width_x * width_y * depth_z * lax.axis_size("col")) ** (-0.5)
    potential_blocks = (summed * factor).astype(BF16)
    block_total = hmask.shape[0]
    blocks_wide = block_total // lax.axis_size("col")
    row_start = lax.axis_index("row") * blocks_here
    col_start = lax.axis_index("col") * blocks_wide
    hpattern = lax.dynamic_slice(hmask, (row_start, col_start), (blocks_here, blocks_wide))
    ppattern = lax.dynamic_slice(pmask, (row_start, col_start), (blocks_here, blocks_wide))
    masked_h = (
        hamiltonian.reshape(blocks_here, BLK, blocks_wide, BLK)
        * hpattern[:, None, :, None].astype(BF16)
    ).reshape(blocks_here * BLK, blocks_wide * BLK)
    masked_p = (
        density.reshape(2, blocks_here, BLK, blocks_wide, BLK)
        * ppattern[None, :, None, :, None].astype(BF16)
    ).reshape(2, blocks_here * BLK, blocks_wide * BLK)

    def diagonal_term(operand):
        local = jnp.einsum(
            "kab,skbc->skac",
            potential_blocks,
            operand.reshape(2, blocks_here, BLK, operand.shape[2]),
            preferred_element_type=F32,
        )
        return local.reshape(2, blocks_here * BLK, operand.shape[2])

    def apply(operand):
        column_whole = lax.all_gather(operand, "row", axis=1, tiled=True)
        remote = jnp.einsum(
            "rk,skc->src",
            lax.all_gather(masked_h, "col", axis=1, tiled=True),
            column_whole,
            preferred_element_type=F32,
        )
        return remote + diagonal_term(operand)

    first = apply(masked_p)
    first_rounded = first.astype(BF16)
    second = apply(first_rounded)
    base = masked_p.astype(F32)
    half_square = 0.5 * TIME_STEP * TIME_STEP
    real_part = base[0] + TIME_STEP * first[1] - half_square * second[0]
    imag_part = base[1] - TIME_STEP * first[0] - half_square * second[1]
    stacked = jnp.stack([real_part, imag_part]).reshape(2, blocks_here, BLK, blocks_wide, BLK)
    stacked = stacked * ppattern[None, :, None, :, None].astype(F32)
    return stacked.reshape(2, blocks_here * BLK, blocks_wide * BLK).astype(BF16)


def solution(mesh):
    in_specs = (
        P("row", "col", None),
        P("row", "col", None, None),
        P("row", "col"),
        P(None, "row", "col"),
        P(),
        P(),
    )
    out_specs = P(None, "row", "col")
    body = shards if (mesh.shape["row"], mesh.shape["col"]) == (8, 4) else gathered
    return jax.shard_map(body, mesh=mesh, in_specs=in_specs, out_specs=out_specs, check_vma=False)
```

```python
import functools

import jax
import jax.numpy as jnp
from jax import lax
from jax.experimental import pallas as pl
from jax.experimental.pallas import tpu as pltpu
from jax.sharding import PartitionSpec as P

BLK = 128
KAPPA = 0.4
TIME_STEP = 0.5
BF16 = jnp.bfloat16
F32 = jnp.float32
VMEM_BYTES = 48 * 1024 * 1024

SMEM_SPEC = pl.BlockSpec(memory_space=pltpu.SMEM)
VMEM_SPEC = pl.BlockSpec(memory_space=pltpu.VMEM)


def call(body, scalars, arrays, outs, scratch=(), flops=0, weight=1):
    moved = sum(a.size * a.dtype.itemsize for a in arrays)
    moved += sum(o.size * o.dtype.itemsize for o in outs)
    return pl.pallas_call(
        body,
        out_shape=tuple(outs),
        in_specs=[SMEM_SPEC] * len(scalars) + [VMEM_SPEC] * len(arrays),
        out_specs=tuple(VMEM_SPEC for _ in outs),
        scratch_shapes=list(scratch),
        compiler_params=pltpu.CompilerParams(vmem_limit_bytes=VMEM_BYTES),
        cost_estimate=pl.CostEstimate(flops=flops, bytes_accessed=weight * moved, transcendentals=0),
    )(*scalars, *arrays)


def shape(*dims, dtype=BF16):
    return jax.ShapeDtypeStruct(dims, dtype)


def kept(mask, row, start, kb, width):
    place = jnp.int32(0)
    for k in range(kb):
        for j in range(width):
            keep = mask[row * kb + k, start + j] != 0
            yield k, j, keep, place
            place = place + keep.astype(jnp.int32)


def pack_kernel(cap, kb, jb, info, hmask, h, h_core, quarter, packed, slots):
    core = info[1] % 2
    for k, j, _, place in kept(hmask, info[0], (info[1] - core) * jb, kb, 2 * jb):
        columns = slice(j % jb * BLK, (j % jb + 1) * BLK)
        block = jnp.where(core == j // jb, h[k * BLK : (k + 1) * BLK, columns], h_core[k * BLK : (k + 1) * BLK, columns])
        here = jnp.clip(place - core * cap, -1, cap) + 1
        slots[pl.ds(pl.multiple_of(here * BLK, BLK), BLK), :] = block
    packed[: cap * BLK, :] = slots[BLK : (cap + 1) * BLK, :]
    packed[cap * BLK :, :] = quarter[...]


def turn_kernel(cap, zs, kb, jb, info, pmask, p, *rest):
    pieces, turned = rest[:-1], rest[-1]
    wide = BLK // zs
    for k, j, _, place in kept(pmask, info[0], info[1] * jb, kb, jb):
        for part in range(2):
            here = p[part, k * BLK : (k + 1) * BLK, j * BLK : (j + 1) * BLK]
            top = pl.multiple_of((2 * place + part) * BLK, BLK)
            turned[pl.ds(top, BLK), :] = here.T
    for s in range(zs):
        start = pl.multiple_of(((info[0] // 2) ^ s) * wide, wide)
        for i in range(2 * cap):
            pieces[s][i * wide : (i + 1) * wide, :] = turned[pl.ds(i * BLK + start, wide), :]


def return_kernel(cap, zs, kb, jb, info, pmask, p, *rest):
    pieces, out, turned = rest[:zs], rest[zs], rest[zs + 1]
    wide = BLK // zs
    for s in range(zs):
        start = pl.multiple_of(((info[0] // 2) ^ s) * wide, wide)
        for i in range(2 * cap):
            turned[pl.ds(i * BLK + start, wide), :] = pieces[s][i * wide : (i + 1) * wide, :]
    for k, j, keep, place in kept(pmask, info[0], info[1] * jb, kb, jb):
        for part in range(2):
            block = (part, slice(k * BLK, (k + 1) * BLK), slice(j * BLK, (j + 1) * BLK))
            top = pl.multiple_of((2 * jnp.minimum(place, cap - 1) + part) * BLK, BLK)
            both = p[block].astype(F32) + turned[pl.ds(top, BLK), :].T.astype(F32)
            out[block] = jnp.where(keep, both, jnp.zeros_like(both)).astype(BF16)


def unpack_kernel(cap, zs, kb, jb, info, pmask, *rest):
    out = rest[-1]
    wide = BLK // zs
    for s in range(zs):
        for other in range(2):
            piece, base = (rest[zs], s * 2 * cap * wide) if other else (rest[s], 0)
            row = info[0] ^ (2 * s + other)
            for k, j, keep, place in kept(pmask, row, info[1] * jb, kb, jb):
                columns = pl.ds(pl.multiple_of((row * kb + k) * BLK, BLK), BLK)
                for part in range(2):
                    top = pl.multiple_of(base + (2 * jnp.minimum(place, cap - 1) + part) * wide, wide)
                    here = piece[pl.ds(top, wide), :]
                    rows = slice((part * jb + j) * wide, (part * jb + j + 1) * wide)
                    out[rows, columns] = jnp.where(keep, here, jnp.zeros_like(here))


def join_kernel(zs, side, info, *rest):
    out = rest[-1]
    for i in range(2 * zs):
        out[:, pl.ds(pl.multiple_of((info[0] ^ i) * side, side), side)] = rest[i][...]


def spread_kernel(s, cap, kb, jb, info, hmask, *rest):
    packed, (dense, diagonal, slots) = rest[:-3], rest[-3:]
    row = info[0] ^ (2 * s)
    part = kb * BLK // 4
    for m in range(4):
        col = info[1] ^ m
        start = pl.multiple_of(col % 2 * (cap * BLK), BLK)
        slots[pl.ds(start, cap * BLK), :] = packed[m][: cap * BLK, :]
        start = pl.multiple_of((2 * (col % 2) + col // 2) * part, part)
        diagonal[pl.ds(start, part), :] = packed[m][cap * BLK :, :]
        if m % 2 == 0:
            continue
        left = col // 2 * (2 * jb)
        for k, j, keep, place in kept(hmask, row, left, kb, 2 * jb):
            source = pl.multiple_of(jnp.minimum(place, 2 * cap - 1) * BLK, BLK)
            start = pl.multiple_of((left + j) * BLK, BLK)
            here = slots[pl.ds(source, BLK), :]
            dense[k * BLK : (k + 1) * BLK, pl.ds(start, BLK)] = jnp.where(keep, here, jnp.zeros_like(here))
    for k in range(kb):
        rows = pl.ds(k * BLK, BLK)
        columns = pl.ds(pl.multiple_of((row * kb + k) * BLK, BLK), BLK)
        both = dense[rows, columns].astype(F32) + diagonal[k * BLK : (k + 1) * BLK, :].astype(F32)
        dense[rows, columns] = both.astype(BF16)


def integral_kernel(effective, basis, total):
    width_x, width_y = effective.shape[:2]
    for k in range(total.shape[0] // BLK):
        rows = slice(k * BLK, (k + 1) * BLK)
        for x in range(width_x):
            for y in range(width_y):
                values = basis[x, y, rows, :]
                weighted = (values.astype(F32) * effective[x, y : y + 1, :]).astype(BF16)
                here = lax.dot_general(weighted, values, (((1,), (1,)), ((), ())), preferred_element_type=F32)
                total[rows, :] = here if x + y == 0 else total[rows, :] + here


def first_kernel(joined, dense, first):
    first[...] = lax.dot_general(
        joined[...], dense[...], (((1,), (1,)), ((), ())), preferred_element_type=F32
    ).astype(BF16)


def second_kernel(slots, cap, zs, kb, jb, info, pmask, joined, *rest):
    half_square = 0.5 * TIME_STEP * TIME_STEP
    count = len(slots)
    dense, first, packed, (change, room) = rest[:count], rest[count : 2 * count], rest[2 * count : -2], rest[-2:]
    wide = BLK // zs
    for i, s in enumerate(slots):
        second = lax.dot_general(
            joined[...], dense[i][...], (((1,), (1,)), ((), ())), preferred_element_type=F32
        )
        half = second.shape[0] // 2
        real, imag = slice(0, half), slice(half, 2 * half)
        other = first[i]
        change[i, real, :] = (TIME_STEP * other[imag, :].astype(F32) - half_square * second[real, :]).astype(BF16)
        change[i, imag, :] = (-TIME_STEP * other[real, :].astype(F32) - half_square * second[imag, :]).astype(BF16)
        for k, j, _, place in kept(pmask, info[0] ^ (2 * s), info[1] * jb, kb, jb):
            for part in range(2):
                top = pl.multiple_of((2 * place + part) * wide, wide)
                rows = slice((part * jb + j) * wide, (part * jb + j + 1) * wide)
                room[i, pl.ds(top, wide), :] = change[i, rows, k * BLK : (k + 1) * BLK]
        packed[i][...] = room[i, : 2 * cap * wide, :]


def swap_row(value, bits):
    count = lax.axis_size("row")
    return lax.ppermute(value, "row", [(i, i ^ bits) for i in range(count)])


def swap_col(value, bits):
    count = lax.axis_size("col")
    return lax.ppermute(value, "col", [(i, i ^ bits) for i in range(count)])


def along(value, pairs):
    return lax.ppermute(value, "row", [(2 * a + x, 2 * b + x) for a, b in pairs for x in range(2)])


def after(done, *values):
    return lax.optimization_barrier((values, done))[0]


def effective_potential(potential):
    def beyond(axis, dim):
        count = lax.axis_size(axis)
        forward = [(i, i + 1) for i in range(count - 1)]
        backward = [(target, source) for source, target in forward]
        last = potential.shape[dim] - 1
        low = lax.ppermute(lax.slice_in_dim(potential, last, None, axis=dim), axis, forward)
        high = lax.ppermute(lax.slice_in_dim(potential, 0, 1, axis=dim), axis, backward)
        return jnp.concatenate([low, potential, high], axis=dim)

    in_x, in_y = beyond("row", 0), beyond("col", 1)
    in_z = jnp.pad(potential, ((0, 0), (0, 0), (1, 1)))
    beside = in_x[2:] + in_x[:-2]
    beside = beside + in_y[:, 2:] + in_y[:, :-2]
    beside = beside + in_z[:, :, 2:] + in_z[:, :, :-2]
    return potential + KAPPA * (beside - 6.0 * potential)


def potential_blocks(potential, basis, gate):
    width_x, width_y, depth_z = potential.shape
    kb = basis.shape[2] // BLK
    effective = effective_potential(potential)
    (total,) = call(
        integral_kernel,
        [],
        [effective, basis],
        [shape(kb * BLK, BLK, dtype=F32)],
        flops=2 * basis.size * BLK,
        weight=32,
    )
    (total,) = after(gate, total)
    part = total.shape[0] // 4

    def of(col):
        return lax.dynamic_slice_in_dim(total, (2 * (col % 2) + col // 2) * part, part, axis=0)

    col = lax.axis_index("col")
    total = of(col) + swap_col(of(col ^ 1), 1) + swap_col(of(col ^ 2), 2) + swap_col(of(col ^ 3), 3)
    factor = float(BLK * width_x * width_y * depth_z * lax.axis_size("col")) ** (-0.5)
    return (total * factor).astype(BF16)


def step(cap, cap_h, potential, basis, hamiltonian, density, hmask, pmask):
    row, col = lax.axis_index("row"), lax.axis_index("col")
    info = jnp.stack([row, col]).astype(jnp.int32)
    z = row // 2
    zs = lax.axis_size("row") // 2
    side, across = hamiltonian.shape
    order = side * lax.axis_size("row")
    kb, jb = side // BLK, across // BLK
    wide = 2 * across // zs
    piece = shape(2 * cap * BLK // zs, BLK)

    pieces = call(
        functools.partial(turn_kernel, cap, zs, kb, jb),
        [info, pmask],
        [density],
        [piece] * zs,
        scratch=[pltpu.VMEM((2 * (kb * jb + 1) * BLK, BLK), BF16)],
    )

    mine = [pieces[s] if s == 0 else swap_row(pieces[s], 2 * s) for s in range(zs)]
    theirs = swap_row(jnp.concatenate(mine), 1)
    hamiltonian_core = swap_col(hamiltonian, 1)
    quarter = potential_blocks(potential, basis, (mine[1], mine[2], mine[3]))
    (own,) = call(
        functools.partial(pack_kernel, cap_h, kb, jb),
        [info, hmask],
        [hamiltonian, hamiltonian_core, quarter],
        [shape(cap_h * BLK + side // 4, BLK)],
        scratch=[pltpu.VMEM(((cap_h + 2) * BLK, BLK), BF16)],
    )

    def spread(s, near, near_core, far, far_core):
        return call(
            functools.partial(spread_kernel, s, cap_h, kb, jb),
            [info, hmask],
            [near, near_core, far, far_core],
            [shape(side, order)],
            scratch=[pltpu.VMEM((side, BLK), BF16), pltpu.VMEM((2 * cap_h * BLK, BLK), BF16)],
        )[0]

    def multiply(rows_of_g):
        return call(
            first_kernel, [], [joined, rows_of_g], [shape(wide, side)], flops=2 * side * order * wide
        )[0]

    middle, outward = [(1, 2), (2, 1)], [(1, 0), (2, 3)]
    inner = (z == 1) | (z == 2)
    beside, over, own_y = swap_row(own, 2), along(own, middle), swap_col(own, 2)

    own, beside, over, own_y = after((over, own_y), own, beside, over, own_y)
    over_beside, out_near, beside_y = along(beside, middle), along(over, outward), swap_col(beside, 2)
    own_core, own_y_core = swap_col(own, 1), swap_col(own_y, 1)
    (joined,) = call(
        functools.partial(unpack_kernel, cap, zs, kb, jb),
        [info, pmask],
        [*mine, theirs],
        [shape(wide, order)],
    )

    dense, first, first_x = [None] * zs, [None] * zs, [None] * zs
    dense[0] = spread(0, own, own_core, own_y, own_y_core)
    first[0] = multiply(dense[0])

    done = (out_near, beside_y, first[0])
    beside, over, over_beside, out_near, beside_y = after(
        done, beside, over, over_beside, out_near, beside_y
    )
    slot_2 = jnp.where(inner, over_beside, out_near)
    out_far, slot_2_y = along(over_beside, outward), swap_col(slot_2, 2)
    beside_core, beside_y_core = swap_col(beside, 1), swap_col(beside_y, 1)
    first_x[0] = swap_row(first[0], 1)
    dense[1] = spread(1, beside, beside_core, beside_y, beside_y_core)
    first[1] = multiply(dense[1])

    done = (out_far, slot_2_y, first[1], first_x[0])
    over, out_far, slot_2, slot_2_y = after(done, over, out_far, slot_2, slot_2_y)
    slot_3 = jnp.where(inner, over, out_far)
    slot_3_y, slot_2_y_core = swap_col(slot_3, 2), swap_col(slot_2_y, 1)
    slot_2_core, slot_3_core = swap_col(slot_2, 1), swap_col(slot_3, 1)
    first_x[1] = swap_row(first[1], 1)
    dense[2] = spread(2, slot_2, slot_2_core, slot_2_y, slot_2_y_core)
    first[2] = multiply(dense[2])
    first_x[2] = swap_row(first[2], 1)

    (slot_3_y,) = after((first_x[1], first[2], slot_3_core), slot_3_y)
    slot_3_y_core = swap_col(slot_3_y, 1)
    dense[3] = spread(3, slot_3, slot_3_core, slot_3_y, slot_3_y_core)
    first[3] = multiply(dense[3])
    first_x[3] = swap_row(first[3], 1)
    (first_joined,) = call(
        functools.partial(join_kernel, zs, side),
        [info],
        [f for pair in zip(first, first_x) for f in pair],
        [shape(wide, order)],
    )

    result = [None] * zs
    for slots in ((3,), (2,), (1,), (0,)):
        outs = call(
            functools.partial(second_kernel, slots, cap, zs, kb, jb),
            [info, pmask],
            [first_joined, *(dense[s] for s in slots), *(first[s] for s in slots)],
            [piece] * len(slots),
            scratch=[
                pltpu.VMEM((len(slots), wide, side), BF16),
                pltpu.VMEM((len(slots), 2 * (kb * jb + 1) * BLK // zs, BLK), BF16),
            ],
            flops=2 * side * order * wide * len(slots),
        )
        for s, out in zip(slots, outs):
            result[s] = out if s == 0 else swap_row(out, 2 * s)

    return call(
        functools.partial(return_kernel, cap, zs, kb, jb),
        [info, pmask],
        [density, *result],
        [shape(2, side, across)],
        scratch=[pltpu.VMEM((2 * cap * BLK, BLK), BF16)],
    )[0]


def shards(potential, basis, hamiltonian, density, hmask, pmask):
    side, across = hamiltonian.shape
    kb, jb = side // BLK, across // BLK

    def most(mask, width):
        return mask.reshape(mask.shape[0] // kb, kb, mask.shape[1] // width, width).sum((1, 3)).max()

    cap, cap_h = kb * jb - 2, kb * jb - 4
    arguments = (potential, basis, hamiltonian, density, hmask, pmask)
    result = step(cap, cap_h, *arguments)
    more = (most(pmask, jb) > cap) | (most(hmask, 2 * jb) > 2 * cap_h)
    return lax.while_loop(
        lambda state: state[0],
        lambda state: (jnp.array(False), step(kb * jb, kb * jb, *arguments)),
        (more, result),
    )[1]


def extended_2(block, sides, width):
    for axis, dim in sides:
        count = lax.axis_size(axis)
        forward = [(i, i + 1) for i in range(count - 1)]
        backward = [(target, source) for source, target in forward]
        low = lax.ppermute(
            lax.slice_in_dim(block, block.shape[dim] - width, None, axis=dim), axis, forward
        )
        high = lax.ppermute(lax.slice_in_dim(block, 0, width, axis=dim), axis, backward)
        block = jnp.concatenate([low, block, high], axis=dim)
    return block


def gathered(potential, basis, hamiltonian, density, hmask, pmask):
    width_x, width_y, depth_z = potential.shape
    extended = extended_2(potential, (("row", 0), ("col", 1)), 1)
    padded = jnp.pad(extended, ((0, 0), (0, 0), (1, 1)))
    beside = padded[2:, 1:-1, 1:-1] + padded[:-2, 1:-1, 1:-1]
    beside = beside + padded[1:-1, 2:, 1:-1] + padded[1:-1, :-2, 1:-1]
    beside = beside + padded[1:-1, 1:-1, 2:] + padded[1:-1, 1:-1, :-2]
    effective = potential + KAPPA * (beside - 6.0 * potential)
    blocks_here = basis.shape[2] // BLK
    weighted = (basis * effective[:, :, None, :]).astype(BF16)
    partial_blocks = jnp.einsum(
        "xykaz,xykbz->kab",
        weighted.reshape(width_x, width_y, blocks_here, BLK, depth_z),
        basis.reshape(width_x, width_y, blocks_here, BLK, depth_z),
        preferred_element_type=F32,
    )
    summed = lax.psum(partial_blocks, "col")
    factor = float(BLK * width_x * width_y * depth_z * lax.axis_size("col")) ** (-0.5)
    potential_blocks = (summed * factor).astype(BF16)
    block_total = hmask.shape[0]
    blocks_wide = block_total // lax.axis_size("col")
    row_start = lax.axis_index("row") * blocks_here
    col_start = lax.axis_index("col") * blocks_wide
    hpattern = lax.dynamic_slice(hmask, (row_start, col_start), (blocks_here, blocks_wide))
    ppattern = lax.dynamic_slice(pmask, (row_start, col_start), (blocks_here, blocks_wide))
    masked_h = (
        hamiltonian.reshape(blocks_here, BLK, blocks_wide, BLK)
        * hpattern[:, None, :, None].astype(BF16)
    ).reshape(blocks_here * BLK, blocks_wide * BLK)
    masked_p = (
        density.reshape(2, blocks_here, BLK, blocks_wide, BLK)
        * ppattern[None, :, None, :, None].astype(BF16)
    ).reshape(2, blocks_here * BLK, blocks_wide * BLK)

    def diagonal_term(operand):
        local = jnp.einsum(
            "kab,skbc->skac",
            potential_blocks,
            operand.reshape(2, blocks_here, BLK, operand.shape[2]),
            preferred_element_type=F32,
        )
        return local.reshape(2, blocks_here * BLK, operand.shape[2])

    def apply(operand):
        column_whole = lax.all_gather(operand, "row", axis=1, tiled=True)
        remote = jnp.einsum(
            "rk,skc->src",
            lax.all_gather(masked_h, "col", axis=1, tiled=True),
            column_whole,
            preferred_element_type=F32,
        )
        return remote + diagonal_term(operand)

    first = apply(masked_p)
    first_rounded = first.astype(BF16)
    second = apply(first_rounded)
    base = masked_p.astype(F32)
    half_square = 0.5 * TIME_STEP * TIME_STEP
    real_part = base[0] + TIME_STEP * first[1] - half_square * second[0]
    imag_part = base[1] - TIME_STEP * first[0] - half_square * second[1]
    stacked = jnp.stack([real_part, imag_part]).reshape(2, blocks_here, BLK, blocks_wide, BLK)
    stacked = stacked * ppattern[None, :, None, :, None].astype(F32)
    return stacked.reshape(2, blocks_here * BLK, blocks_wide * BLK).astype(BF16)


def solution(mesh):
    in_specs = (
        P("row", "col", None),
        P("row", "col", None, None),
        P("row", "col"),
        P(None, "row", "col"),
        P(),
        P(),
    )
    out_specs = P(None, "row", "col")
    body = shards if (mesh.shape["row"], mesh.shape["col"]) == (8, 4) else gathered
    return jax.shard_map(body, mesh=mesh, in_specs=in_specs, out_specs=out_specs, check_vma=False)
```

```python
import functools

import jax
import jax.numpy as jnp
from jax import lax
from jax.experimental import pallas as pl
from jax.experimental.pallas import tpu as pltpu
from jax.sharding import PartitionSpec as P

BLK = 128
KAPPA = 0.4
TIME_STEP = 0.5
BF16 = jnp.bfloat16
F32 = jnp.float32
VMEM_BYTES = 48 * 1024 * 1024

SMEM_SPEC = pl.BlockSpec(memory_space=pltpu.SMEM)
VMEM_SPEC = pl.BlockSpec(memory_space=pltpu.VMEM)


def call(body, scalars, arrays, outs, scratch=(), flops=0, weight=1):
    moved = sum(a.size * a.dtype.itemsize for a in arrays)
    moved += sum(o.size * o.dtype.itemsize for o in outs)
    return pl.pallas_call(
        body,
        out_shape=tuple(outs),
        in_specs=[SMEM_SPEC] * len(scalars) + [VMEM_SPEC] * len(arrays),
        out_specs=tuple(VMEM_SPEC for _ in outs),
        scratch_shapes=list(scratch),
        compiler_params=pltpu.CompilerParams(vmem_limit_bytes=VMEM_BYTES),
        cost_estimate=pl.CostEstimate(flops=flops, bytes_accessed=weight * moved, transcendentals=0),
    )(*scalars, *arrays)


def shape(*dims, dtype=BF16):
    return jax.ShapeDtypeStruct(dims, dtype)


def kept(mask, row, start, kb, width):
    place = jnp.int32(0)
    for k in range(kb):
        for j in range(width):
            keep = mask[row * kb + k, start + j] != 0
            yield k, j, keep, place
            place = place + keep.astype(jnp.int32)


def pack_kernel(cap, kb, jb, info, hmask, h, h_core, quarter, packed, slots):
    core = info[1] % 2
    for k, j, _, place in kept(hmask, info[0], (info[1] - core) * jb, kb, 2 * jb):
        columns = slice(j % jb * BLK, (j % jb + 1) * BLK)
        block = jnp.where(core == j // jb, h[k * BLK : (k + 1) * BLK, columns], h_core[k * BLK : (k + 1) * BLK, columns])
        here = jnp.clip(place - core * cap, -1, cap) + 1
        slots[pl.ds(pl.multiple_of(here * BLK, BLK), BLK), :] = block
    packed[: cap * BLK, :] = slots[BLK : (cap + 1) * BLK, :]
    packed[cap * BLK :, :] = quarter[...]


def turn_kernel(cap, zs, kb, jb, info, pmask, p, *rest):
    pieces, turned = rest[:-1], rest[-1]
    wide = BLK // zs
    for k, j, _, place in kept(pmask, info[0], info[1] * jb, kb, jb):
        for part in range(2):
            here = p[part, k * BLK : (k + 1) * BLK, j * BLK : (j + 1) * BLK]
            top = pl.multiple_of((2 * place + part) * BLK, BLK)
            turned[pl.ds(top, BLK), :] = here.T
    for s in range(zs):
        start = pl.multiple_of(((info[0] // 2) ^ s) * wide, wide)
        for i in range(2 * cap):
            pieces[s][i * wide : (i + 1) * wide, :] = turned[pl.ds(i * BLK + start, wide), :]


def return_kernel(cap, zs, kb, jb, info, pmask, p, *rest):
    pieces, out, turned = rest[:zs], rest[zs], rest[zs + 1]
    wide = BLK // zs
    for s in range(zs):
        start = pl.multiple_of(((info[0] // 2) ^ s) * wide, wide)
        for i in range(2 * cap):
            turned[pl.ds(i * BLK + start, wide), :] = pieces[s][i * wide : (i + 1) * wide, :]
    for k, j, keep, place in kept(pmask, info[0], info[1] * jb, kb, jb):
        for part in range(2):
            block = (part, slice(k * BLK, (k + 1) * BLK), slice(j * BLK, (j + 1) * BLK))
            top = pl.multiple_of((2 * jnp.minimum(place, cap - 1) + part) * BLK, BLK)
            both = p[block].astype(F32) + turned[pl.ds(top, BLK), :].T.astype(F32)
            out[block] = jnp.where(keep, both, jnp.zeros_like(both)).astype(BF16)


def unpack_kernel(cap, zs, kb, jb, info, pmask, *rest):
    out = rest[-1]
    wide = BLK // zs
    for s in range(zs):
        for other in range(2):
            piece, base = (rest[zs], s * 2 * cap * wide) if other else (rest[s], 0)
            row = info[0] ^ (2 * s + other)
            for k, j, keep, place in kept(pmask, row, info[1] * jb, kb, jb):
                columns = pl.ds(pl.multiple_of((row * kb + k) * BLK, BLK), BLK)
                for part in range(2):
                    top = pl.multiple_of(base + (2 * jnp.minimum(place, cap - 1) + part) * wide, wide)
                    here = piece[pl.ds(top, wide), :]
                    rows = slice((part * jb + j) * wide, (part * jb + j + 1) * wide)
                    out[rows, columns] = jnp.where(keep, here, jnp.zeros_like(here))


def join_kernel(zs, side, info, *rest):
    out = rest[-1]
    for i in range(2 * zs):
        out[:, pl.ds(pl.multiple_of((info[0] ^ i) * side, side), side)] = rest[i][...]


def spread_kernel(s, cap, kb, jb, info, hmask, *rest):
    joined, packed, (dense, first, diagonal, slots) = rest[0], rest[1:-4], rest[-4:]
    row = info[0] ^ (2 * s)
    part = kb * BLK // 4
    for m in range(4):
        col = info[1] ^ m
        start = pl.multiple_of(col % 2 * (cap * BLK), BLK)
        slots[pl.ds(start, cap * BLK), :] = packed[m][: cap * BLK, :]
        start = pl.multiple_of((2 * (col % 2) + col // 2) * part, part)
        diagonal[pl.ds(start, part), :] = packed[m][cap * BLK :, :]
        if m % 2 == 0:
            continue
        left = col // 2 * (2 * jb)
        for k, j, keep, place in kept(hmask, row, left, kb, 2 * jb):
            source = pl.multiple_of(jnp.minimum(place, 2 * cap - 1) * BLK, BLK)
            start = pl.multiple_of((left + j) * BLK, BLK)
            here = slots[pl.ds(source, BLK), :]
            dense[k * BLK : (k + 1) * BLK, pl.ds(start, BLK)] = jnp.where(keep, here, jnp.zeros_like(here))
    for k in range(kb):
        rows = pl.ds(k * BLK, BLK)
        columns = pl.ds(pl.multiple_of((row * kb + k) * BLK, BLK), BLK)
        both = dense[rows, columns].astype(F32) + diagonal[k * BLK : (k + 1) * BLK, :].astype(F32)
        dense[rows, columns] = both.astype(BF16)
    first[...] = lax.dot_general(
        joined[...], dense[...], (((1,), (1,)), ((), ())), preferred_element_type=F32
    ).astype(BF16)


def integral_kernel(effective, basis, total):
    width_x, width_y = effective.shape[:2]
    for k in range(total.shape[0] // BLK):
        rows = slice(k * BLK, (k + 1) * BLK)
        for x in range(width_x):
            for y in range(width_y):
                values = basis[x, y, rows, :]
                weighted = (values.astype(F32) * effective[x, y : y + 1, :]).astype(BF16)
                here = lax.dot_general(weighted, values, (((1,), (1,)), ((), ())), preferred_element_type=F32)
                total[rows, :] = here if x + y == 0 else total[rows, :] + here


def second_kernel(slots, cap, zs, kb, jb, info, pmask, joined, *rest):
    half_square = 0.5 * TIME_STEP * TIME_STEP
    count = len(slots)
    dense, first, packed, (change, room) = rest[:count], rest[count : 2 * count], rest[2 * count : -2], rest[-2:]
    wide = BLK // zs
    for i, s in enumerate(slots):
        second = lax.dot_general(
            joined[...], dense[i][...], (((1,), (1,)), ((), ())), preferred_element_type=F32
        )
        half = second.shape[0] // 2
        real, imag = slice(0, half), slice(half, 2 * half)
        other = first[i]
        change[i, real, :] = (TIME_STEP * other[imag, :].astype(F32) - half_square * second[real, :]).astype(BF16)
        change[i, imag, :] = (-TIME_STEP * other[real, :].astype(F32) - half_square * second[imag, :]).astype(BF16)
        for k, j, _, place in kept(pmask, info[0] ^ (2 * s), info[1] * jb, kb, jb):
            for part in range(2):
                top = pl.multiple_of((2 * place + part) * wide, wide)
                rows = slice((part * jb + j) * wide, (part * jb + j + 1) * wide)
                room[i, pl.ds(top, wide), :] = change[i, rows, k * BLK : (k + 1) * BLK]
        packed[i][...] = room[i, : 2 * cap * wide, :]


def swap_row(value, bits):
    count = lax.axis_size("row")
    return lax.ppermute(value, "row", [(i, i ^ bits) for i in range(count)])


def swap_col(value, bits):
    count = lax.axis_size("col")
    return lax.ppermute(value, "col", [(i, i ^ bits) for i in range(count)])


def along(value, pairs):
    return lax.ppermute(value, "row", [(2 * a + x, 2 * b + x) for a, b in pairs for x in range(2)])


def after(done, *values):
    return lax.optimization_barrier((values, done))[0]


def effective_potential(potential):
    def beyond(axis, dim):
        count = lax.axis_size(axis)
        forward = [(i, i + 1) for i in range(count - 1)]
        backward = [(target, source) for source, target in forward]
        last = potential.shape[dim] - 1
        low = lax.ppermute(lax.slice_in_dim(potential, last, None, axis=dim), axis, forward)
        high = lax.ppermute(lax.slice_in_dim(potential, 0, 1, axis=dim), axis, backward)
        return jnp.concatenate([low, potential, high], axis=dim)

    in_x, in_y = beyond("row", 0), beyond("col", 1)
    in_z = jnp.pad(potential, ((0, 0), (0, 0), (1, 1)))
    beside = in_x[2:] + in_x[:-2]
    beside = beside + in_y[:, 2:] + in_y[:, :-2]
    beside = beside + in_z[:, :, 2:] + in_z[:, :, :-2]
    return potential + KAPPA * (beside - 6.0 * potential)


def potential_blocks(potential, basis, gate):
    width_x, width_y, depth_z = potential.shape
    kb = basis.shape[2] // BLK
    effective = effective_potential(potential)
    (total,) = call(
        integral_kernel,
        [],
        [effective, basis],
        [shape(kb * BLK, BLK, dtype=F32)],
        flops=2 * basis.size * BLK,
        weight=32,
    )
    (total,) = after(gate, total)
    part = total.shape[0] // 4

    def of(col):
        return lax.dynamic_slice_in_dim(total, (2 * (col % 2) + col // 2) * part, part, axis=0)

    col = lax.axis_index("col")
    total = of(col) + swap_col(of(col ^ 1), 1) + swap_col(of(col ^ 2), 2) + swap_col(of(col ^ 3), 3)
    factor = float(BLK * width_x * width_y * depth_z * lax.axis_size("col")) ** (-0.5)
    return (total * factor).astype(BF16)


def step(cap, cap_h, potential, basis, hamiltonian, density, hmask, pmask):
    row, col = lax.axis_index("row"), lax.axis_index("col")
    info = jnp.stack([row, col]).astype(jnp.int32)
    z = row // 2
    zs = lax.axis_size("row") // 2
    side, across = hamiltonian.shape
    order = side * lax.axis_size("row")
    kb, jb = side // BLK, across // BLK
    wide = 2 * across // zs
    piece = shape(2 * cap * BLK // zs, BLK)

    pieces = call(
        functools.partial(turn_kernel, cap, zs, kb, jb),
        [info, pmask],
        [density],
        [piece] * zs,
        scratch=[pltpu.VMEM((2 * (kb * jb + 1) * BLK, BLK), BF16)],
    )

    mine = [pieces[s] if s == 0 else swap_row(pieces[s], 2 * s) for s in range(zs)]
    theirs = swap_row(jnp.concatenate(mine), 1)
    hamiltonian_core = swap_col(hamiltonian, 1)
    quarter = potential_blocks(potential, basis, (mine[1], mine[2], mine[3]))
    (own,) = call(
        functools.partial(pack_kernel, cap_h, kb, jb),
        [info, hmask],
        [hamiltonian, hamiltonian_core, quarter],
        [shape(cap_h * BLK + side // 4, BLK)],
        scratch=[pltpu.VMEM(((cap_h + 2) * BLK, BLK), BF16)],
    )

    def spread(s, near, near_core, far, far_core):
        return call(
            functools.partial(spread_kernel, s, cap_h, kb, jb),
            [info, hmask],
            [joined, near, near_core, far, far_core],
            [shape(side, order), shape(wide, side)],
            scratch=[pltpu.VMEM((side, BLK), BF16), pltpu.VMEM((2 * cap_h * BLK, BLK), BF16)],
            flops=2 * side * order * wide,
        )

    middle, outward = [(1, 2), (2, 1)], [(1, 0), (2, 3)]
    inner = (z == 1) | (z == 2)
    beside, over, own_y = swap_row(own, 2), along(own, middle), swap_col(own, 2)

    own, beside, over, own_y = after((over, own_y), own, beside, over, own_y)
    over_beside, out_near, beside_y = along(beside, middle), along(over, outward), swap_col(beside, 2)
    own_core, own_y_core = swap_col(own, 1), swap_col(own_y, 1)
    (joined,) = call(
        functools.partial(unpack_kernel, cap, zs, kb, jb),
        [info, pmask],
        [*mine, theirs],
        [shape(wide, order)],
    )

    dense, first, first_x = [None] * zs, [None] * zs, [None] * zs
    dense[0], first[0] = spread(0, own, own_core, own_y, own_y_core)

    done = (out_near, beside_y, first[0])
    beside, over, over_beside, out_near, beside_y = after(
        done, beside, over, over_beside, out_near, beside_y
    )
    slot_2 = jnp.where(inner, over_beside, out_near)
    out_far, slot_2_y = along(over_beside, outward), swap_col(slot_2, 2)
    beside_core, beside_y_core = swap_col(beside, 1), swap_col(beside_y, 1)
    first_x[0] = swap_row(first[0], 1)
    dense[1], first[1] = spread(1, beside, beside_core, beside_y, beside_y_core)

    done = (out_far, slot_2_y, first[1], first_x[0])
    over, out_far, slot_2, slot_2_y = after(done, over, out_far, slot_2, slot_2_y)
    slot_3 = jnp.where(inner, over, out_far)
    slot_3_y, slot_2_y_core = swap_col(slot_3, 2), swap_col(slot_2_y, 1)
    slot_2_core, slot_3_core = swap_col(slot_2, 1), swap_col(slot_3, 1)
    first_x[1] = swap_row(first[1], 1)
    dense[2], first[2] = spread(2, slot_2, slot_2_core, slot_2_y, slot_2_y_core)
    first_x[2] = swap_row(first[2], 1)

    (slot_3_y,) = after((first_x[1], first[2], slot_3_core), slot_3_y)
    slot_3_y_core = swap_col(slot_3_y, 1)
    dense[3], first[3] = spread(3, slot_3, slot_3_core, slot_3_y, slot_3_y_core)
    first_x[3] = swap_row(first[3], 1)
    (first_joined,) = call(
        functools.partial(join_kernel, zs, side),
        [info],
        [f for pair in zip(first, first_x) for f in pair],
        [shape(wide, order)],
    )

    result = [None] * zs
    for slots in ((3,), (2,), (1,), (0,)):
        outs = call(
            functools.partial(second_kernel, slots, cap, zs, kb, jb),
            [info, pmask],
            [first_joined, *(dense[s] for s in slots), *(first[s] for s in slots)],
            [piece] * len(slots),
            scratch=[
                pltpu.VMEM((len(slots), wide, side), BF16),
                pltpu.VMEM((len(slots), 2 * (kb * jb + 1) * BLK // zs, BLK), BF16),
            ],
            flops=2 * side * order * wide * len(slots),
        )
        for s, out in zip(slots, outs):
            result[s] = out if s == 0 else swap_row(out, 2 * s)

    return call(
        functools.partial(return_kernel, cap, zs, kb, jb),
        [info, pmask],
        [density, *result],
        [shape(2, side, across)],
        scratch=[pltpu.VMEM((2 * cap * BLK, BLK), BF16)],
    )[0]


def shards(potential, basis, hamiltonian, density, hmask, pmask):
    side, across = hamiltonian.shape
    kb, jb = side // BLK, across // BLK

    def most(mask, width):
        return mask.reshape(mask.shape[0] // kb, kb, mask.shape[1] // width, width).sum((1, 3)).max()

    cap, cap_h = kb * jb - 2, kb * jb - 4
    arguments = (potential, basis, hamiltonian, density, hmask, pmask)
    result = step(cap, cap_h, *arguments)
    more = (most(pmask, jb) > cap) | (most(hmask, 2 * jb) > 2 * cap_h)
    return lax.while_loop(
        lambda state: state[0],
        lambda state: (jnp.array(False), step(kb * jb, kb * jb, *arguments)),
        (more, result),
    )[1]


def extended_2(block, sides, width):
    for axis, dim in sides:
        count = lax.axis_size(axis)
        forward = [(i, i + 1) for i in range(count - 1)]
        backward = [(target, source) for source, target in forward]
        low = lax.ppermute(
            lax.slice_in_dim(block, block.shape[dim] - width, None, axis=dim), axis, forward
        )
        high = lax.ppermute(lax.slice_in_dim(block, 0, width, axis=dim), axis, backward)
        block = jnp.concatenate([low, block, high], axis=dim)
    return block


def gathered(potential, basis, hamiltonian, density, hmask, pmask):
    width_x, width_y, depth_z = potential.shape
    extended = extended_2(potential, (("row", 0), ("col", 1)), 1)
    padded = jnp.pad(extended, ((0, 0), (0, 0), (1, 1)))
    beside = padded[2:, 1:-1, 1:-1] + padded[:-2, 1:-1, 1:-1]
    beside = beside + padded[1:-1, 2:, 1:-1] + padded[1:-1, :-2, 1:-1]
    beside = beside + padded[1:-1, 1:-1, 2:] + padded[1:-1, 1:-1, :-2]
    effective = potential + KAPPA * (beside - 6.0 * potential)
    blocks_here = basis.shape[2] // BLK
    weighted = (basis * effective[:, :, None, :]).astype(BF16)
    partial_blocks = jnp.einsum(
        "xykaz,xykbz->kab",
        weighted.reshape(width_x, width_y, blocks_here, BLK, depth_z),
        basis.reshape(width_x, width_y, blocks_here, BLK, depth_z),
        preferred_element_type=F32,
    )
    summed = lax.psum(partial_blocks, "col")
    factor = float(BLK * width_x * width_y * depth_z * lax.axis_size("col")) ** (-0.5)
    potential_blocks = (summed * factor).astype(BF16)
    block_total = hmask.shape[0]
    blocks_wide = block_total // lax.axis_size("col")
    row_start = lax.axis_index("row") * blocks_here
    col_start = lax.axis_index("col") * blocks_wide
    hpattern = lax.dynamic_slice(hmask, (row_start, col_start), (blocks_here, blocks_wide))
    ppattern = lax.dynamic_slice(pmask, (row_start, col_start), (blocks_here, blocks_wide))
    masked_h = (
        hamiltonian.reshape(blocks_here, BLK, blocks_wide, BLK)
        * hpattern[:, None, :, None].astype(BF16)
    ).reshape(blocks_here * BLK, blocks_wide * BLK)
    masked_p = (
        density.reshape(2, blocks_here, BLK, blocks_wide, BLK)
        * ppattern[None, :, None, :, None].astype(BF16)
    ).reshape(2, blocks_here * BLK, blocks_wide * BLK)

    def diagonal_term(operand):
        local = jnp.einsum(
            "kab,skbc->skac",
            potential_blocks,
            operand.reshape(2, blocks_here, BLK, operand.shape[2]),
            preferred_element_type=F32,
        )
        return local.reshape(2, blocks_here * BLK, operand.shape[2])

    def apply(operand):
        column_whole = lax.all_gather(operand, "row", axis=1, tiled=True)
        remote = jnp.einsum(
            "rk,skc->src",
            lax.all_gather(masked_h, "col", axis=1, tiled=True),
            column_whole,
            preferred_element_type=F32,
        )
        return remote + diagonal_term(operand)

    first = apply(masked_p)
    first_rounded = first.astype(BF16)
    second = apply(first_rounded)
    base = masked_p.astype(F32)
    half_square = 0.5 * TIME_STEP * TIME_STEP
    real_part = base[0] + TIME_STEP * first[1] - half_square * second[0]
    imag_part = base[1] - TIME_STEP * first[0] - half_square * second[1]
    stacked = jnp.stack([real_part, imag_part]).reshape(2, blocks_here, BLK, blocks_wide, BLK)
    stacked = stacked * ppattern[None, :, None, :, None].astype(F32)
    return stacked.reshape(2, blocks_here * BLK, blocks_wide * BLK).astype(BF16)


def solution(mesh):
    in_specs = (
        P("row", "col", None),
        P("row", "col", None, None),
        P("row", "col"),
        P(None, "row", "col"),
        P(),
        P(),
    )
    out_specs = P(None, "row", "col")
    body = shards if (mesh.shape["row"], mesh.shape["col"]) == (8, 4) else gathered
    return jax.shard_map(body, mesh=mesh, in_specs=in_specs, out_specs=out_specs, check_vma=False)
```
